256 devices in a mesh: row: 32 (over z, y_hi, core), col: 8 (over x, y_lo).
Axes of the slice: x: 4, y: 4 (y_hi: 2, y_lo: 2; y = y_hi * 2 + y_lo), z: 8, core: 2. Of those that a mesh axis runs over, the one named last changes fastest.
Arguments:
- covariance: float32 [16384, 16384], P('row', 'col'), may hold values from -6 to 10
- rotations: bfloat16 [2048, 16384], P(None, 'row'), may hold values from -1 to 2
Outputs:
- rotated: bfloat16 [16384, 16384], P('row', 'col')
The draws below stay inside these ranges and needn't reach their ends.
All inputs are finite; a program needn't handle non-finite values.
Results may differ from the reference program's by a relative error of at most 0.0049.
Values may be sent and summed in bfloat16 or wider, within the bound.
A program may use at most 128 MiB of HBM per device.

```python
import jax
import jax.numpy as jnp
import numpy as np
from jax import lax

PAIR = 2048
PAIRS = 8
ORDER = 16384


def draw_covariance(key, part):
    key = jax.random.fold_in(key, 11)
    first, second = jax.random.split(key, 2)
    raw = jax.random.truncated_normal(first, -6.0, 6.0, (ORDER, ORDER), jnp.float32)
    upper = jnp.triu(raw)
    symmetric = upper + jnp.triu(raw, 1).T
    shift = jax.random.uniform(second, (ORDER,), jnp.float32, 2.0, 4.0)
    return symmetric + jnp.diag(shift)


def draw_rotations(key, part):
    key = jax.random.fold_in(key, 23)
    rows_pos = jnp.arange(PAIR)[:, None]
    cols_pos = jnp.arange(PAIRS * PAIR)[None, :] % PAIR
    identity = (rows_pos == cols_pos).astype(jnp.float32)
    noise = jax.random.truncated_normal(key, -6.0, 6.0, (PAIR, PAIRS * PAIR), jnp.float32)
    return (identity + noise * (0.5 / PAIR ** 0.5)).astype(jnp.bfloat16)


def setup_inputs(seed: int = 0) -> dict:
    seeds = jax.random.split(jax.random.key(seed), 3)
    covariance = draw_covariance(jax.random.fold_in(seeds[2], 71), 0)
    rotations = draw_rotations(jax.random.fold_in(seeds[2], 71), 0)
    return dict(covariance=covariance, rotations=rotations)


def tournament(pairs):
    source = list(range(2 * pairs))
    source[0] = 0
    source[2] = 1
    for index in range(2, pairs):
        source[2 * index] = 2 * index - 2
    for index in range(pairs - 1):
        source[2 * index + 1] = 2 * index + 3
    source[2 * pairs - 1] = 2 * pairs - 2
    return np.array(source, dtype=np.int32)


def reference(covariance, rotations):
    tile = PAIR // 2
    blocks = rotations.astype(jnp.float32).reshape(PAIR, PAIRS, PAIR).transpose(1, 0, 2)
    strips = covariance.reshape(ORDER, PAIRS, PAIR)
    turned = jnp.einsum("npk,pkj->npj", strips, blocks, precision=lax.Precision.HIGHEST)
    turned = turned.astype(jnp.bfloat16).reshape(ORDER, 2 * PAIRS, tile)
    source = tournament(PAIRS)
    moved = turned[:, source, :].reshape(ORDER, ORDER)
    grouped = moved.astype(jnp.float32).reshape(PAIRS, PAIR, ORDER)
    rows = jnp.einsum("pkj,pkn->pjn", blocks, grouped, precision=lax.Precision.HIGHEST)
    rows = rows.astype(jnp.bfloat16).reshape(2 * PAIRS, tile, ORDER)
    return rows[source].reshape(ORDER, ORDER)
```

```python
import functools

import jax
import jax.numpy as jnp
from jax import lax
from jax.experimental import pallas as pl
from jax.experimental.pallas import tpu as pltpu
from jax.sharding import PartitionSpec as P

MESH = pl.DeviceIdType.MESH
PLANES = 8
COLUMNS = 8
XS = 4
BF16 = jnp.bfloat16


def row_of(z, hi, k):
    return z * 4 + hi * 2 + k


def kernel(
    c_ref,
    m_ref,
    o_ref,
    c_raw,
    m_raw,
    c_all,
    m_t,
    m_q,
    t_out,
    t_in,
    y_out,
    c_load,
    m_load,
    c_send,
    c_recv,
    p_send,
    p_recv,
    v_send,
    v_recv,
    x_send,
    x_recv,
    s_send,
    s_recv,
    g_send,
    g_recv,
    t_send,
    t_recv,
    y_send,
    y_recv,
):
    rows, pair = c_ref.shape
    width = m_ref.shape[1]
    piece = width // 4
    half = pair // 2
    small = piece // 2
    tile = pair // 2

    r = lax.axis_index("row")
    c = lax.axis_index("col")
    z, hi, k = r // 4, r // 2 % 2, r % 2
    x, lo = c // 2, c % 2

    mate = (row_of(z, hi, 1 - k), c)
    z_next = (row_of((z + 1) % PLANES, hi, k), c)
    z_prev = (row_of((z + PLANES - 1) % PLANES, hi, k), c)
    across = (row_of(z, 1 - hi, k), x * 2 + 1 - lo)
    x_next = (r, (x + 1) % XS * 2 + lo)
    x_prev = (r, (x + XS - 1) % XS * 2 + lo)

    out_piece = x // 2 * 4 + hi * 2 + x % 2
    out_hi = jnp.where(lo == z % 2, hi, 1 - hi)
    scatter_to = (row_of(out_piece, out_hi, k), z)
    scatter_self = (out_piece == z) & (out_hi == hi) & (z == c)
    in_hi = z // 2 % 2
    in_x = z // 4 * 2 + z % 2
    in_lo = jnp.where(hi == in_hi, c % 2, 1 - c % 2)
    scatter_from = (row_of(c, in_hi, k), in_x * 2 + in_lo)

    t_col = (
        jnp.where(c == 0, 0, jnp.where(c == COLUMNS - 1, c, c + 1)),
        jnp.where(c == 0, 1, c - 1),
    )
    t_slot = (jnp.where(c == COLUMNS - 1, 1, 0), jnp.where(c == 0, 0, 1))
    src_col = jnp.where(
        hi == 0,
        jnp.where(c <= 1, 0, c - 1),
        jnp.where(c == COLUMNS - 1, c, c + 1),
    )
    src_tile = jnp.where(
        hi == 0, jnp.where(c == 1, 1, 0), jnp.where(c == COLUMNS - 1, 0, 1)
    )

    y_z = (
        jnp.where(z == 0, 0, jnp.where(z == PLANES - 1, z, z + 1)),
        jnp.where(z == 0, 1, z - 1),
    )
    y_hi = (jnp.where(z == PLANES - 1, 1, 0), jnp.where(z == 0, 0, 1))
    src_z = jnp.where(
        hi == 0,
        jnp.where(z <= 1, 0, z - 1),
        jnp.where(z == PLANES - 1, z, z + 1),
    )

    barrier = pltpu.get_barrier_semaphore()

    def greet(device):
        pl.semaphore_signal(barrier, inc=1, device_id=device, device_id_type=MESH)

    for device in (mate, z_next, z_prev, across, x_next, x_prev):
        greet(device)
    expected = jnp.int32(6)

    @pl.when(jnp.logical_not(scatter_self))
    def _():
        greet(scatter_from)

    expected = expected + jnp.where(scatter_self, 0, 1)
    for source_hi in range(2):
        device = (row_of(z, source_hi, k), src_col)

        @pl.when((src_col != c) | (hi != source_hi))
        def _():
            greet(device)

    for b in range(2):
        expected = expected + jnp.where((t_col[b] == c) & (t_slot[b] == hi), 0, 1)
    for source_hi in range(2):
        for source_k in range(2):
            device = (row_of(src_z, source_hi, source_k), c)

            @pl.when((src_z != z) | (hi != source_hi) | (k != source_k))
            def _():
                greet(device)

    for b in range(2):
        for h in range(2):
            stays = (y_z[b] == z) & (y_hi[b] == hi) & (k == h)
            expected = expected + jnp.where(stays, 0, 1)

    def remote(src, dst, send, recv, device):
        return pltpu.make_async_remote_copy(
            src_ref=src,
            dst_ref=dst,
            send_sem=send,
            recv_sem=recv,
            device_id=device,
            device_id_type=MESH,
        )

    c_step = rows // 4

    def c_copy(i):
        at = pl.ds(i * c_step, c_step)
        return pltpu.make_async_copy(c_ref.at[at], c_raw.at[at], c_load.at[i])

    m_copy = pltpu.make_async_copy(m_ref, m_raw, m_load)
    m_copy.start()
    for i in range(4):
        c_copy(i).start()

    pl.semaphore_wait(barrier, expected)

    def scatter(h):
        at = pl.ds(h * half, half)
        src = m_ref.at[at, pl.ds(pl.multiple_of(x * piece, piece), piece)]
        return remote(
            src, m_q.at[out_piece, at], s_send.at[h], s_recv.at[h], scatter_to
        )

    def scatter_local(h):
        at = pl.ds(h * half, half)
        src = m_ref.at[at, pl.ds(pl.multiple_of(x * piece, piece), piece)]
        return pltpu.make_async_copy(src, m_q.at[z, at], s_recv.at[h])

    def scatter_in(h):
        at = pl.ds(h * half, half)
        ref = m_q.at[z, at]
        return remote(ref, ref, s_send.at[h], s_recv.at[h], mate)

    @pl.when(scatter_self)
    def _():
        for h in range(2):
            scatter_local(h).start()

    @pl.when(jnp.logical_not(scatter_self))
    def _():
        for h in range(2):
            scatter(h).start()

    m_copy.wait()
    shard = hi * 2 + k
    other = (1 - hi) * 2 + k
    mate_other = (1 - hi) * 2 + 1 - k

    def t_rows(which, quarter, count=piece, start=0):
        at = pl.multiple_of(which * width + quarter * piece + start, small)
        return m_t.at[pl.ds(at, count)]

    def turn(quarter):
        cols = pl.ds(pl.multiple_of(quarter * piece, piece), piece)
        to = pl.ds(pl.multiple_of(shard * width + quarter * piece, piece), piece)
        m_t[to, :] = m_raw[:, cols].T

    to_across = remote(
        t_rows(shard, x), t_rows(shard, x), v_send, v_recv, across
    )
    from_across = remote(
        t_rows(other, x), t_rows(other, x), v_send, v_recv, across
    )
    turn(x)
    to_across.start()

    def c_rows(core, i):
        at = pl.multiple_of(core * rows + i * c_step, c_step)
        return c_all.at[pl.ds(at, c_step)]

    def c_out(i):
        return remote(c_rows(k, i), c_rows(k, i), c_send.at[i], c_recv.at[i], mate)

    def c_in(i):
        ref = c_rows(1 - k, i)
        return remote(ref, ref, c_send.at[i], c_recv.at[i], mate)

    for i in range(4):
        c_copy(i).wait()
        at = pl.multiple_of(k * rows + i * c_step, c_step)
        c_all[pl.ds(at, c_step), :] = c_raw[pl.ds(i * c_step, c_step), :].astype(BF16)
        c_out(i).start()

    for step in range(1, 4):
        turn((x + step) % XS)
    own = pl.ds(pl.multiple_of(shard * width, width), width)
    shard_out = remote(m_t.at[own], m_t.at[own], p_send.at[0], p_recv.at[0], mate)
    shard_out.start()
    mates = pl.ds(
        pl.multiple_of((hi * 2 + 1 - k) * width, width), width
    )
    shard_in = remote(m_t.at[mates], m_t.at[mates], p_send.at[0], p_recv.at[0], mate)

    def relay(i, quarter):
        ref = t_rows(other, quarter)
        return remote(ref, ref, p_send.at[i], p_recv.at[i], mate)

    def relay_in(i, quarter):
        ref = t_rows(mate_other, quarter)
        return remote(ref, ref, p_send.at[i], p_recv.at[i], mate)

    def x_near(way, quarter):
        ref = t_rows(other, quarter)
        device = (x_next, x_prev)[way]
        return remote(ref, ref, x_send.at[way, 0], x_recv.at[way, 0], device)

    def x_far(way, quarter):
        ref = t_rows(other, quarter, small, way * small)
        device = (x_next, x_prev)[way]
        return remote(ref, ref, x_send.at[way, 1], x_recv.at[way, 1], device)

    x_behind = ((x + XS - 1) % XS, (x + 1) % XS)
    x_two = (x + 2) % XS

    def ring(way, distance, h):
        j = ((z + PLANES - distance) % PLANES, (z + distance) % PLANES)[way]
        ref = m_q.at[j, pl.ds(h * half, half)]
        device = (z_next, z_prev)[way]
        at = (way, distance, h)
        return remote(ref, ref, g_send.at[at], g_recv.at[at], device)

    def ring_in(way, distance, h):
        j = ((z + PLANES - distance) % PLANES, (z + distance) % PLANES)[way]
        ref = m_q.at[j, pl.ds(h * half, half)]
        at = (way, distance - 1, h)
        return remote(ref, ref, g_send.at[at], g_recv.at[at], z_next)

    def tile_of(j):
        return j // 2 % 2, j // 4 * 2 + j % 2

    def first(pieces, slot):
        step = min(256, 2 * rows)
        count = len(pieces)

        @pl.loop(0, 2 * rows // step)
        def _(i):
            at = pl.ds(pl.multiple_of(i * step, step), step)
            right = [m_q[j] for j in pieces]
            right = right[0] if count == 1 else jnp.concatenate(right, axis=1)
            got = jnp.dot(c_all[at, :], right, preferred_element_type=jnp.float32)
            got = got.astype(BF16)
            for n in range(count):
                t_out[slot + n, at, :] = got[:, n * piece : (n + 1) * piece]

        for n, j in enumerate(pieces):
            copy, local, away = t_copies(j, slot + n)

            @pl.when(away)
            def _():
                copy.start()

            @pl.when(jnp.logical_not(away))
            def _():
                local.start()

    def t_copies(j, slot):
        b, chunk = tile_of(j)
        col = jnp.where(b == 0, t_col[0], t_col[1])
        to = jnp.where(b == 0, t_slot[0], t_slot[1])
        dst = t_in.at[chunk, pl.ds(pl.multiple_of(hi * tile, tile), tile)]
        recv = t_recv.at[chunk, hi]
        copy = remote(
            t_out.at[slot], dst, t_send.at[slot], recv, (row_of(z, to, k), col)
        )
        local = pltpu.make_async_copy(t_out.at[slot], dst, recv)
        away = (col != c) | (to != hi)
        return copy, local, away

    def y_copies(chunk, b, h):
        g = b * 2 + h
        src = y_out.at[chunk, pl.ds(g * width, width)]
        start = hi * tile + k * width + chunk * piece
        dst = o_ref.at[:, pl.ds(pl.multiple_of(start, piece), piece)]
        recv = y_recv.at[hi, k, chunk]
        device = (row_of(y_z[b], y_hi[b], h), c)
        copy = remote(src, dst, y_send.at[chunk, g], recv, device)
        local = pltpu.make_async_copy(src, dst, recv)
        away = (y_z[b] != z) | (y_hi[b] != hi) | (k != h)
        return copy, local, away

    def second(j):
        tile_index, chunk = tile_of(j)

        @pl.when(tile_index == src_tile)
        def _():
            for source in range(2):
                ref = t_in.at[chunk, pl.ds(source * tile, tile)]
                remote(
                    ref, ref, t_send.at[0], t_recv.at[chunk, source], mate
                ).wait_recv()
            step = min(256, width)
            for b in range(2):
                for h in range(2):
                    base = (b * 2 + h) * width

                    @pl.loop(0, width // step)
                    def _(i):
                        at = pl.ds(pl.multiple_of(base + i * step, step), step)
                        got = jnp.dot(
                            m_t[at, :],
                            t_in[chunk],
                            preferred_element_type=jnp.float32,
                        )
                        y_out[chunk, at, :] = got.astype(BF16)

                    copy, local, away = y_copies(chunk, b, h)

                    @pl.when(away)
                    def _():
                        copy.start()

                    @pl.when(jnp.logical_not(away))
                    def _():
                        local.start()

    for h in range(2):
        scatter_in(h).wait_recv()
        for way in range(2):
            ring(way, 0, h).start()
    for i in range(4):
        c_in(i).wait_recv()
    first([z], 0)
    from_across.wait_recv()
    for way in range(2):
        x_near(way, x).start()
    relay(1, x).start()

    for distance in range(1, 4):
        for h in range(2):
            for way in range(2):
                ring_in(way, distance, h).wait_recv()
                if distance < 3 or h == way:
                    ring(way, distance, h).start()
        ahead, behind = (z + distance) % PLANES, (z + PLANES - distance) % PLANES
        first([behind, ahead], 2 * distance - 1)
        if distance == 1:
            for way in range(2):
                x_near(way, x_behind[way]).wait_recv()
                x_far(way, x_behind[way]).start()
                relay(2 + way, x_behind[way]).start()
        if distance == 2:
            for way in range(2):
                x_far(way, x_two).wait_recv()
            relay(4, x_two).start()
            shard_in.wait_recv()
            for i, quarter in enumerate((x, x_behind[0], x_behind[1], x_two)):
                relay_in(1 + i, quarter).wait_recv()
            second(z)
        if distance >= 2:
            second((z + PLANES - distance + 1) % PLANES)
            second((z + distance - 1) % PLANES)
    for way in range(2):
        ring_in(way, 4, way).wait_recv()
    first([(z + 4) % PLANES], 7)
    second((z + PLANES - 3) % PLANES)
    second((z + 3) % PLANES)
    second((z + 4) % PLANES)

    @pl.when(jnp.logical_not(scatter_self))
    def _():
        for h in range(2):
            scatter(h).wait_send()

    to_across.wait_send()
    shard_out.wait_send()
    for i in range(4):
        c_out(i).wait_send()
    for i, quarter in enumerate((x, x_behind[0], x_behind[1], x_two)):
        relay(1 + i, quarter).wait_send()
    for way in range(2):
        x_near(way, x).wait_send()
        x_far(way, x_behind[way]).wait_send()
        for distance in range(4):
            for h in range(2):
                if distance < 3 or h == way:
                    ring(way, distance, h).wait_send()
    order = [z]
    for distance in range(1, 4):
        order += [(z + PLANES - distance) % PLANES, (z + distance) % PLANES]
    order += [(z + 4) % PLANES]
    for slot, j in enumerate(order):
        copy, local, away = t_copies(j, slot)

        @pl.when(away)
        def _():
            copy.wait_send()

    for chunk in range(4):
        for b in range(2):
            for h in range(2):
                copy, local, away = y_copies(chunk, b, h)

                @pl.when(away)
                def _():
                    copy.wait_send()

    for source_hi in range(2):
        for source_k in range(2):
            for chunk in range(4):
                start = source_hi * tile + source_k * width + chunk * piece
                ref = o_ref.at[:, pl.ds(start, piece)]
                remote(
                    ref, ref, t_send.at[0], y_recv.at[source_hi, source_k, chunk], mate
                ).wait_recv()


def shards(covariance, rotations):
    rows, pair = covariance.shape
    width = rotations.shape[1]
    piece = width // 4
    dma = pltpu.SemaphoreType.DMA
    return pl.pallas_call(
        kernel,
        out_shape=jax.ShapeDtypeStruct((rows, pair), BF16),
        in_specs=[pl.BlockSpec(memory_space=pl.ANY)] * 2,
        out_specs=pl.BlockSpec(memory_space=pl.ANY),
        scratch_shapes=[
            pltpu.VMEM((rows, pair), jnp.float32),
            pltpu.VMEM((pair, width), BF16),
            pltpu.VMEM((2 * rows, pair), BF16),
            pltpu.VMEM((pair, pair), BF16),
            pltpu.VMEM((PLANES, pair, piece), BF16),
            pltpu.VMEM((PLANES, 2 * rows, piece), BF16),
            pltpu.VMEM((4, pair, piece), BF16),
            pltpu.VMEM((4, pair, piece), BF16),
            dma((4,)),
            dma,
            dma((4,)),
            dma((4,)),
            dma((5,)),
            dma((5,)),
            dma,
            dma,
            dma((2, 2)),
            dma((2, 2)),
            dma((2,)),
            dma((2,)),
            dma((2, 4, 2)),
            dma((2, 4, 2)),
            dma((PLANES,)),
            dma((4, 2)),
            dma((4, 4)),
            dma((2, 2, 4)),
        ],
        compiler_params=pltpu.CompilerParams(
            collective_id=0,
            has_side_effects=True,
            vmem_limit_bytes=56 * 1024 * 1024,
        ),
        cost_estimate=pl.CostEstimate(
            flops=4 * rows * pair * pair, bytes_accessed=8 * rows * pair, transcendentals=0
        ),
    )(covariance, rotations)


def solution(mesh):
    placed = (P("row", "col"), P(None, "row"))
    return jax.shard_map(
        shards, mesh=mesh, in_specs=placed, out_specs=P("row", "col"), check_vma=False
    )
```

```python
import functools

import jax
import jax.numpy as jnp
from jax import lax
from jax.experimental import pallas as pl
from jax.experimental.pallas import tpu as pltpu
from jax.sharding import PartitionSpec as P

MESH = pl.DeviceIdType.MESH
PLANES = 8
COLUMNS = 8
XS = 4
BF16 = jnp.bfloat16


def row_of(z, hi, k):
    return z * 4 + hi * 2 + k


CHUNKS = 16
SLACK = 2
C_CHUNKS = 8


def kernel(
    c_ref,
    m_ref,
    o_ref,
    c_raw,
    m_raw,
    c_all,
    m_t,
    m_q,
    turned_in,
    t_all,
    y_out,
    c_load,
    m_load,
    q_load,
    c_send,
    c_recv,
    e_send,
    e_recv,
    f_send,
    f_recv,
    p_send,
    p_recv,
    v_send,
    v_recv,
    x_send,
    x_recv,
    r_send,
    r_recv,
    g_send,
    g_recv,
    y_send,
    y_recv,
):
    rows, pair = c_ref.shape
    width = m_ref.shape[1]
    piece = width // 4
    half = pair // 2
    tile = pair // 2

    r = lax.axis_index("row")
    c = lax.axis_index("col")
    z, hi, k = r // 4, r // 2 % 2, r % 2
    x, lo = c // 2, c % 2

    mate = (row_of(z, hi, 1 - k), c)
    twin = (row_of(z, 1 - hi, k), c)
    z_next = (row_of((z + 1) % PLANES, hi, k), c)
    z_prev = (row_of((z + PLANES - 1) % PLANES, hi, k), c)
    across = (row_of(z, 1 - hi, k), x * 2 + 1 - lo)
    x_others = [(r, (x + n) % XS * 2 + lo) for n in range(1, XS)]

    last = COLUMNS - 1
    to_col = jnp.where(
        hi == 0,
        jnp.where(c == 0, 0, jnp.where(c == last, c, c + 1)),
        jnp.where(c == 0, 1, c - 1),
    )
    to_slot = jnp.where(hi == 0, jnp.where(c == last, 1, 0), jnp.where(c == 0, 0, 1))
    src_col = (jnp.where(c <= 1, 0, c - 1), jnp.where(c == last, c, c + 1))
    src_tile = (jnp.where(c == 1, 1, 0), jnp.where(c == last, 0, 1))

    y_z = (
        jnp.where(z == 0, 0, jnp.where(z == PLANES - 1, z, z + 1)),
        jnp.where(z == 0, 1, z - 1),
    )
    y_hi = (jnp.where(z == PLANES - 1, 1, 0), jnp.where(z == 0, 0, 1))
    src_z = jnp.where(
        hi == 0,
        jnp.where(z <= 1, 0, z - 1),
        jnp.where(z == PLANES - 1, z, z + 1),
    )

    barrier = pltpu.get_barrier_semaphore()

    def greet(device):
        pl.semaphore_signal(barrier, inc=1, device_id=device, device_id_type=MESH)

    for device in (mate, twin, z_next, z_prev, across, *x_others):
        greet(device)
    expected = jnp.int32(8)
    for slot in range(2):
        for h in range(2):
            same = (src_z == z) & (src_tile[slot] == hi) & (h == k)
            same = same & (src_col[slot] == c)
            device = (row_of(src_z, src_tile[slot], h), src_col[slot])

            @pl.when(jnp.logical_not(same))
            def _():
                greet(device)

    def stays(b, h):
        return (y_z[b] == z) & (y_hi[b] == hi) & (h == k) & (to_col == c)

    for b in range(2):
        for h in range(2):
            expected = expected + jnp.where(stays(b, h), 0, 1)

    def remote(src, dst, send, recv, device):
        return pltpu.make_async_remote_copy(
            src_ref=src,
            dst_ref=dst,
            send_sem=send,
            recv_sem=recv,
            device_id=device,
            device_id_type=MESH,
        )

    c_step = rows // C_CHUNKS

    def c_copy(i):
        at = pl.ds(i * c_step, c_step)
        return pltpu.make_async_copy(c_ref.at[at], c_raw.at[at], c_load.at[i])

    up = (z - c + PLANES) % PLANES
    down = (c - z + PLANES) % PLANES
    m_copy = pltpu.make_async_copy(m_ref, m_raw, m_load)
    q_copy = pltpu.make_async_copy(m_ref, m_q, q_load)

    @pl.when(up == 0)
    def _():
        q_copy.start()

    for i in range(C_CHUNKS):
        c_copy(i).start()
    m_copy.start()

    pl.semaphore_wait(barrier, expected)

    def over(part):
        at = pl.ds(part * half, half)
        src = m_ref.at[at, pl.ds(pl.multiple_of(x * piece, piece), piece)]
        return remote(
            src, turned_in.at[at], v_send.at[part], v_recv.at[part], across
        )

    for part in range(2):
        over(part).start()

    def c_rows(of_hi, core, i):
        at = pl.multiple_of(of_hi * tile + core * rows + i * c_step, c_step)
        return c_all.at[pl.ds(at, c_step)]

    def c_mate(i):
        ref = c_rows(hi, k, i)
        return remote(ref, ref, c_send.at[i], c_recv.at[i], mate)

    def c_mate_in(i):
        ref = c_rows(hi, 1 - k, i)
        return remote(ref, ref, c_send.at[i], c_recv.at[i], mate)

    def c_twin(i):
        ref = c_rows(hi, k, i)
        return remote(ref, ref, e_send.at[i], e_recv.at[i], twin)

    def c_twin_in(i):
        ref = c_rows(1 - hi, k, i)
        return remote(ref, ref, e_send.at[i], e_recv.at[i], twin)

    def c_relay(i):
        ref = c_rows(1 - hi, k, i)
        return remote(ref, ref, f_send.at[i], f_recv.at[i], mate)

    def c_relay_in(i):
        ref = c_rows(1 - hi, 1 - k, i)
        return remote(ref, ref, f_send.at[i], f_recv.at[i], mate)

    for part in range(2):
        over(part).wait_recv()
    for i in range(C_CHUNKS):
        c_copy(i).wait()
        at = pl.multiple_of(hi * tile + k * rows + i * c_step, c_step)
        c_all[pl.ds(at, c_step), :] = c_raw[pl.ds(i * c_step, c_step), :].astype(BF16)
        c_twin(i).start()

    @pl.when(up == 0)
    def _():
        q_copy.wait()

    q_step = half // CHUNKS

    def spread(way, n):
        at = pl.multiple_of(way * half + n * q_step, q_step)
        ref = m_q.at[pl.ds(at, q_step)]
        device = (z_next, z_prev)[way]
        return remote(ref, ref, g_send.at[way, n], g_recv.at[way, n], device)

    def pass_on(s):
        for way, distance in ((0, up), (1, down)):
            n = s - SLACK * distance
            here = (n >= 0) & (n < CHUNKS)

            @pl.when(here & (distance > 0))
            def _():
                spread(way, n).wait_recv()

            @pl.when(here & (distance < PLANES - 1))
            def _():
                spread(way, n).start()

    every = 4

    def slots(first, end):
        @pl.loop(first, end)
        def _(s):
            pass_on(s)

            @pl.when((s % every == every - 1) & (s < every * C_CHUNKS))
            def _():
                i = s // every
                c_twin_in(i).wait_recv()
                c_relay(i).start()

    slots(0, 2)

    m_copy.wait()
    shard = hi * 2 + k
    other = (1 - hi) * 2 + k
    mate_other = (1 - hi) * 2 + 1 - k

    def t_rows(which, quarter):
        return pl.ds(pl.multiple_of(which * width + quarter * piece, piece), piece)

    for i in range(C_CHUNKS):
        c_mate(i).start()
    for quarter in range(4):
        m_t[t_rows(shard, quarter), :] = m_raw[
            :, quarter * piece : (quarter + 1) * piece
        ].T
    own = pl.ds(pl.multiple_of(shard * width, width), width)
    shard_out = remote(m_t.at[own], m_t.at[own], p_send, p_recv, mate)
    shard_out.start()
    mates = pl.ds(pl.multiple_of((hi * 2 + 1 - k) * width, width), width)
    shard_in = remote(m_t.at[mates], m_t.at[mates], p_send, p_recv, mate)

    def along(n, part):
        ref = m_t.at[t_rows(other, x), pl.ds(part * half, half)]
        at = (n - 1, part)
        return remote(ref, ref, x_send.at[at], x_recv.at[at], x_others[n - 1])

    def along_in(n, part):
        quarter = (x + XS - n) % XS
        ref = m_t.at[t_rows(other, quarter), pl.ds(part * half, half)]
        at = (n - 1, part)
        return remote(ref, ref, x_send.at[at], x_recv.at[at], mate)

    def relay(n, part, of=other):
        quarter = (x + XS - n) % XS
        ref = m_t.at[t_rows(of, quarter), pl.ds(part * half, half)]
        return remote(ref, ref, r_send.at[n, part], r_recv.at[n, part], mate)

    def turn_over(part):
        at = slice(part * half, (part + 1) * half)
        m_t[t_rows(other, x), at] = turned_in[at, :].T
        for n in range(1, XS):
            along(n, part).start()
        relay(0, part).start()

    slots(2, 14)
    turn_over(0)
    slots(14, 24)
    turn_over(1)
    slots(24, CHUNKS + SLACK * (PLANES - 1))

    def first(start, count):
        step = min(256, count)

        @pl.loop(0, count // step)
        def _(i):
            at = pl.ds(pl.multiple_of(start + i * step, step), step)
            got = jnp.dot(c_all[at, :], m_q[...], preferred_element_type=jnp.float32)
            t_all[at, :] = got.astype(BF16)

    for i in range(C_CHUNKS):
        c_mate_in(i).wait_recv()
    first(hi * tile, tile)
    left = (CHUNKS + SLACK * (PLANES - 1)) // every
    for i in range(left, C_CHUNKS):
        c_twin_in(i).wait_recv()
        c_relay(i).start()
    first((1 - hi) * tile + k * rows, rows)
    for i in range(C_CHUNKS):
        c_relay_in(i).wait_recv()
    first((1 - hi) * tile + (1 - k) * rows, rows)
    for part in range(2):
        for n in range(1, XS):
            along_in(n, part).wait_recv()
            relay(n, part).start()
    shard_in.wait_recv()
    for part in range(2):
        for n in range(XS):
            relay(n, part, mate_other).wait_recv()

    def y_copies(b, h):
        src = y_out.at[pl.ds((b * 2 + h) * width, width)]
        place = to_slot * tile + k * width
        dst = o_ref.at[:, pl.ds(pl.multiple_of(place, width), width)]
        recv = y_recv.at[to_slot, k]
        device = (row_of(y_z[b], y_hi[b], h), to_col)
        copy = remote(src, dst, y_send.at[b, h], recv, device)
        return copy, pltpu.make_async_copy(src, dst, recv)

    for b in range(2):
        for h in range(2):
            base = (b * 2 + h) * width
            step = min(256, width)

            @pl.loop(0, width // step)
            def _(i):
                at = pl.ds(pl.multiple_of(base + i * step, step), step)
                got = jnp.dot(m_t[at, :], t_all[...], preferred_element_type=jnp.float32)
                y_out[at, :] = got.astype(BF16)

            copy, local = y_copies(b, h)

            @pl.when(jnp.logical_not(stays(b, h)))
            def _():
                copy.start()

            @pl.when(stays(b, h))
            def _():
                local.start()

    shard_out.wait_send()
    for i in range(C_CHUNKS):
        c_mate(i).wait_send()
        c_twin(i).wait_send()
        c_relay(i).wait_send()
    for part in range(2):
        over(part).wait_send()
        for n in range(XS):
            relay(n, part).wait_send()
        for n in range(1, XS):
            along(n, part).wait_send()

    for way, distance in ((0, up), (1, down)):

        @pl.when(distance < PLANES - 1)
        def _():
            @pl.loop(0, CHUNKS)
            def _(n):
                spread(way, n).wait_send()

    for b in range(2):
        for h in range(2):
            copy, _ = y_copies(b, h)

            @pl.when(jnp.logical_not(stays(b, h)))
            def _():
                copy.wait_send()

    for slot in range(2):
        for h in range(2):
            ref = o_ref.at[:, pl.ds(slot * tile + h * width, width)]
            remote(ref, ref, y_send.at[0, 0], y_recv.at[slot, h], mate).wait_recv()


def shards(covariance, rotations):
    rows, pair = covariance.shape
    width = rotations.shape[1]
    dma = pltpu.SemaphoreType.DMA
    return pl.pallas_call(
        kernel,
        out_shape=jax.ShapeDtypeStruct((rows, pair), BF16),
        in_specs=[pl.BlockSpec(memory_space=pl.ANY)] * 2,
        out_specs=pl.BlockSpec(memory_space=pl.ANY),
        scratch_shapes=[
            pltpu.VMEM((rows, pair), jnp.float32),
            pltpu.VMEM((pair, width), BF16),
            pltpu.VMEM((pair, pair), BF16),
            pltpu.VMEM((pair, pair), BF16),
            pltpu.VMEM((pair, width), BF16),
            pltpu.VMEM((pair, width // 4), BF16),
            pltpu.VMEM((pair, width), BF16),
            pltpu.VMEM((pair, width), BF16),
            dma((C_CHUNKS,)),
            dma,
            dma,
            dma((C_CHUNKS,)),
            dma((C_CHUNKS,)),
            dma((C_CHUNKS,)),
            dma((C_CHUNKS,)),
            dma((C_CHUNKS,)),
            dma((C_CHUNKS,)),
            dma,
            dma,
            dma((2,)),
            dma((2,)),
            dma((XS - 1, 2)),
            dma((XS - 1, 2)),
            dma((XS, 2)),
            dma((XS, 2)),
            dma((2, CHUNKS)),
            dma((2, CHUNKS)),
            dma((2, 2)),
            dma((2, 2)),
        ],
        compiler_params=pltpu.CompilerParams(
            collective_id=0,
            has_side_effects=True,
            vmem_limit_bytes=56 * 1024 * 1024,
        ),
        cost_estimate=pl.CostEstimate(
            flops=4 * rows * pair * pair, bytes_accessed=8 * rows * pair, transcendentals=0
        ),
    )(covariance, rotations)


def solution(mesh):
    placed = (P("row", "col"), P(None, "row"))
    return jax.shard_map(
        shards, mesh=mesh, in_specs=placed, out_specs=P("row", "col"), check_vma=False
    )
```

```python
import functools

import jax
import jax.numpy as jnp
from jax import lax
from jax.experimental import pallas as pl
from jax.experimental.pallas import tpu as pltpu
from jax.sharding import PartitionSpec as P

MESH = pl.DeviceIdType.MESH
PLANES = 8
COLUMNS = 8
XS = 4
BF16 = jnp.bfloat16


def row_of(z, hi, k):
    return z * 4 + hi * 2 + k


CHUNKS = 16
SLACK = 2
HEAD = 6
EARLY = 6
C_CHUNKS = 8


def kernel(
    c_ref,
    m_ref,
    o_ref,
    c_raw,
    m_raw,
    c_all,
    m_t,
    m_q,
    turned_in,
    t_all,
    y_out,
    c_load,
    m_load,
    q_load,
    c_send,
    c_recv,
    e_send,
    e_recv,
    f_send,
    f_recv,
    p_send,
    p_recv,
    v_send,
    v_recv,
    x_send,
    x_recv,
    r_send,
    r_recv,
    g_send,
    g_recv,
    y_send,
    y_recv,
):
    rows, pair = c_ref.shape
    width = m_ref.shape[1]
    piece = width // 4
    half = pair // 2
    tile = pair // 2

    r = lax.axis_index("row")
    c = lax.axis_index("col")
    z, hi, k = r // 4, r // 2 % 2, r % 2
    x, lo = c // 2, c % 2

    mate = (row_of(z, hi, 1 - k), c)
    twin = (row_of(z, 1 - hi, k), c)
    z_next = (row_of((z + 1) % PLANES, hi, k), c)
    z_prev = (row_of((z + PLANES - 1) % PLANES, hi, k), c)
    across = (row_of(z, 1 - hi, k), x * 2 + 1 - lo)
    x_others = [(r, (x + n) % XS * 2 + lo) for n in range(1, XS)]

    last = COLUMNS - 1
    to_col = jnp.where(
        hi == 0,
        jnp.where(c == 0, 0, jnp.where(c == last, c, c + 1)),
        jnp.where(c == 0, 1, c - 1),
    )
    to_slot = jnp.where(hi == 0, jnp.where(c == last, 1, 0), jnp.where(c == 0, 0, 1))
    src_col = (jnp.where(c <= 1, 0, c - 1), jnp.where(c == last, c, c + 1))
    src_tile = (jnp.where(c == 1, 1, 0), jnp.where(c == last, 0, 1))

    y_z = (
        jnp.where(z == 0, 0, jnp.where(z == PLANES - 1, z, z + 1)),
        jnp.where(z == 0, 1, z - 1),
    )
    y_hi = (jnp.where(z == PLANES - 1, 1, 0), jnp.where(z == 0, 0, 1))
    src_z = jnp.where(
        hi == 0,
        jnp.where(z <= 1, 0, z - 1),
        jnp.where(z == PLANES - 1, z, z + 1),
    )

    barrier = pltpu.get_barrier_semaphore()

    def greet(device):
        pl.semaphore_signal(barrier, inc=1, device_id=device, device_id_type=MESH)

    for device in (mate, twin, z_next, z_prev, across, *x_others):
        greet(device)
    expected = jnp.int32(8)
    for slot in range(2):
        for h in range(2):
            same = (src_z == z) & (src_tile[slot] == hi) & (h == k)
            same = same & (src_col[slot] == c)
            device = (row_of(src_z, src_tile[slot], h), src_col[slot])

            @pl.when(jnp.logical_not(same))
            def _():
                greet(device)

    def stays(b, h):
        return (y_z[b] == z) & (y_hi[b] == hi) & (h == k) & (to_col == c)

    for b in range(2):
        for h in range(2):
            expected = expected + jnp.where(stays(b, h), 0, 1)

    def remote(src, dst, send, recv, device):
        return pltpu.make_async_remote_copy(
            src_ref=src,
            dst_ref=dst,
            send_sem=send,
            recv_sem=recv,
            device_id=device,
            device_id_type=MESH,
        )

    c_step = rows // C_CHUNKS

    def c_copy(i):
        at = pl.ds(i * c_step, c_step)
        return pltpu.make_async_copy(c_ref.at[at], c_raw.at[at], c_load.at[i])

    up = (z - c + PLANES) % PLANES
    down = (c - z + PLANES) % PLANES
    m_copy = pltpu.make_async_copy(m_ref, m_raw, m_load)
    q_copy = pltpu.make_async_copy(m_ref, m_q, q_load)

    @pl.when(up == 0)
    def _():
        q_copy.start()

    for i in range(C_CHUNKS):
        c_copy(i).start()
    m_copy.start()

    pl.semaphore_wait(barrier, expected)

    def over(part):
        at = pl.ds(part * half, half)
        src = m_ref.at[at, pl.ds(pl.multiple_of(x * piece, piece), piece)]
        return remote(
            src, turned_in.at[at], v_send.at[part], v_recv.at[part], across
        )

    for part in range(2):
        over(part).start()

    def c_rows(of_hi, core, i):
        at = pl.multiple_of(of_hi * tile + core * rows + i * c_step, c_step)
        return c_all.at[pl.ds(at, c_step)]

    def c_mate(i):
        ref = c_rows(hi, k, i)
        return remote(ref, ref, c_send.at[i], c_recv.at[i], mate)

    def c_mate_in(i):
        ref = c_rows(hi, 1 - k, i)
        return remote(ref, ref, c_send.at[i], c_recv.at[i], mate)

    def c_twin(i):
        ref = c_rows(hi, k, i)
        return remote(ref, ref, e_send.at[i], e_recv.at[i], twin)

    def c_twin_in(i):
        ref = c_rows(1 - hi, k, i)
        return remote(ref, ref, e_send.at[i], e_recv.at[i], twin)

    def c_relay(i):
        ref = c_rows(1 - hi, k, i)
        return remote(ref, ref, f_send.at[i], f_recv.at[i], mate)

    def c_relay_in(i):
        ref = c_rows(1 - hi, 1 - k, i)
        return remote(ref, ref, f_send.at[i], f_recv.at[i], mate)

    for i in range(C_CHUNKS):
        c_copy(i).wait()
        at = pl.multiple_of(hi * tile + k * rows + i * c_step, c_step)
        c_all[pl.ds(at, c_step), :] = c_raw[pl.ds(i * c_step, c_step), :].astype(BF16)
        c_mate(i).start()

    @pl.when(up == 0)
    def _():
        q_copy.wait()

    q_step = half // CHUNKS

    def spread(way, n):
        at = pl.multiple_of(way * half + n * q_step, q_step)
        ref = m_q.at[pl.ds(at, q_step)]
        device = (z_next, z_prev)[way]
        return remote(ref, ref, g_send.at[way, n], g_recv.at[way, n], device)

    def pass_on(s):
        for way, distance in ((0, up), (1, down)):
            n = s - SLACK * distance
            here = (n >= 0) & (n < CHUNKS)

            @pl.when(here & (distance > 0))
            def _():
                spread(way, n).wait_recv()

            @pl.when(here & (distance < PLANES - 1))
            def _():
                spread(way, n).start()

    every = 4

    def slots(first, end):
        @pl.loop(first, end)
        def _(s):
            pass_on(s)

            n = s - HEAD

            @pl.when((n >= 0) & (n % every == every - 1) & (n < every * EARLY))
            def _():
                i = n // every
                c_twin_in(i).wait_recv()
                c_relay(i).start()

    slots(0, HEAD)

    m_copy.wait()
    shard = hi * 2 + k
    other = (1 - hi) * 2 + k
    mate_other = (1 - hi) * 2 + 1 - k

    def t_rows(which, quarter):
        return pl.ds(pl.multiple_of(which * width + quarter * piece, piece), piece)

    for quarter in range(4):
        m_t[t_rows(shard, quarter), :] = m_raw[
            :, quarter * piece : (quarter + 1) * piece
        ].T
    own = pl.ds(pl.multiple_of(shard * width, width), width)
    shard_out = remote(m_t.at[own], m_t.at[own], p_send, p_recv, mate)
    shard_out.start()
    mates = pl.ds(pl.multiple_of((hi * 2 + 1 - k) * width, width), width)
    shard_in = remote(m_t.at[mates], m_t.at[mates], p_send, p_recv, mate)

    def along(n, part):
        ref = m_t.at[t_rows(other, x), pl.ds(part * half, half)]
        at = (n - 1, part)
        return remote(ref, ref, x_send.at[at], x_recv.at[at], x_others[n - 1])

    def along_in(n, part):
        quarter = (x + XS - n) % XS
        ref = m_t.at[t_rows(other, quarter), pl.ds(part * half, half)]
        at = (n - 1, part)
        return remote(ref, ref, x_send.at[at], x_recv.at[at], mate)

    def relay(n, part, of=other):
        quarter = (x + XS - n) % XS
        ref = m_t.at[t_rows(of, quarter), pl.ds(part * half, half)]
        return remote(ref, ref, r_send.at[n, part], r_recv.at[n, part], mate)

    def turn_over(part):
        at = slice(part * half, (part + 1) * half)
        m_t[t_rows(other, x), at] = turned_in[at, :].T
        for n in range(1, XS):
            along(n, part).start()
        relay(0, part).start()

    for part in range(2):
        over(part).wait_recv()
    for i in range(C_CHUNKS):
        c_twin(i).start()
    for part in range(2):
        turn_over(part)
    slots(HEAD, CHUNKS + SLACK * (PLANES - 1))

    def first(start, count):
        step = min(256, count)

        @pl.loop(0, count // step)
        def _(i):
            at = pl.ds(pl.multiple_of(start + i * step, step), step)
            got = jnp.dot(c_all[at, :], m_q[...], preferred_element_type=jnp.float32)
            t_all[at, :] = got.astype(BF16)

    for i in range(C_CHUNKS):
        c_mate_in(i).wait_recv()
    first(hi * tile, tile)
    group = C_CHUNKS // 2
    part_rows = rows // 2
    for n in range(2):
        for i in range(n * group, (n + 1) * group):
            if i >= EARLY:
                c_twin_in(i).wait_recv()
                c_relay(i).start()
        first((1 - hi) * tile + k * rows + n * part_rows, part_rows)
    for n in range(2):
        for i in range(n * group, (n + 1) * group):
            c_relay_in(i).wait_recv()
        first((1 - hi) * tile + (1 - k) * rows + n * part_rows, part_rows)
    for part in range(2):
        for n in range(1, XS):
            along_in(n, part).wait_recv()
            relay(n, part).start()
    shard_in.wait_recv()
    for part in range(2):
        for n in range(XS):
            relay(n, part, mate_other).wait_recv()

    def y_copies(b, h):
        src = y_out.at[pl.ds((b * 2 + h) * width, width)]
        place = to_slot * tile + k * width
        dst = o_ref.at[:, pl.ds(pl.multiple_of(place, width), width)]
        recv = y_recv.at[to_slot, k]
        device = (row_of(y_z[b], y_hi[b], h), to_col)
        copy = remote(src, dst, y_send.at[b, h], recv, device)
        return copy, pltpu.make_async_copy(src, dst, recv)

    for b in range(2):
        for h in range(2):
            base = (b * 2 + h) * width
            step = min(256, width)

            @pl.loop(0, width // step)
            def _(i):
                at = pl.ds(pl.multiple_of(base + i * step, step), step)
                got = jnp.dot(m_t[at, :], t_all[...], preferred_element_type=jnp.float32)
                y_out[at, :] = got.astype(BF16)

            copy, local = y_copies(b, h)

            @pl.when(jnp.logical_not(stays(b, h)))
            def _():
                copy.start()

            @pl.when(stays(b, h))
            def _():
                local.start()

    shard_out.wait_send()
    for i in range(C_CHUNKS):
        c_mate(i).wait_send()
        c_twin(i).wait_send()
        c_relay(i).wait_send()
    for part in range(2):
        over(part).wait_send()
        for n in range(XS):
            relay(n, part).wait_send()
        for n in range(1, XS):
            along(n, part).wait_send()

    for way, distance in ((0, up), (1, down)):

        @pl.when(distance < PLANES - 1)
        def _():
            @pl.loop(0, CHUNKS)
            def _(n):
                spread(way, n).wait_send()

    for b in range(2):
        for h in range(2):
            copy, _ = y_copies(b, h)

            @pl.when(jnp.logical_not(stays(b, h)))
            def _():
                copy.wait_send()

    for slot in range(2):
        for h in range(2):
            ref = o_ref.at[:, pl.ds(slot * tile + h * width, width)]
            remote(ref, ref, y_send.at[0, 0], y_recv.at[slot, h], mate).wait_recv()


def shards(covariance, rotations):
    rows, pair = covariance.shape
    width = rotations.shape[1]
    dma = pltpu.SemaphoreType.DMA
    return pl.pallas_call(
        kernel,
        out_shape=jax.ShapeDtypeStruct((rows, pair), BF16),
        in_specs=[pl.BlockSpec(memory_space=pl.ANY)] * 2,
        out_specs=pl.BlockSpec(memory_space=pl.ANY),
        scratch_shapes=[
            pltpu.VMEM((rows, pair), jnp.float32),
            pltpu.VMEM((pair, width), BF16),
            pltpu.VMEM((pair, pair), BF16),
            pltpu.VMEM((pair, pair), BF16),
            pltpu.VMEM((pair, width), BF16),
            pltpu.VMEM((pair, width // 4), BF16),
            pltpu.VMEM((pair, width), BF16),
            pltpu.VMEM((pair, width), BF16),
            dma((C_CHUNKS,)),
            dma,
            dma,
            dma((C_CHUNKS,)),
            dma((C_CHUNKS,)),
            dma((C_CHUNKS,)),
            dma((C_CHUNKS,)),
            dma((C_CHUNKS,)),
            dma((C_CHUNKS,)),
            dma,
            dma,
            dma((2,)),
            dma((2,)),
            dma((XS - 1, 2)),
            dma((XS - 1, 2)),
            dma((XS, 2)),
            dma((XS, 2)),
            dma((2, CHUNKS)),
            dma((2, CHUNKS)),
            dma((2, 2)),
            dma((2, 2)),
        ],
        compiler_params=pltpu.CompilerParams(
            collective_id=0,
            has_side_effects=True,
            vmem_limit_bytes=56 * 1024 * 1024,
        ),
        cost_estimate=pl.CostEstimate(
            flops=4 * rows * pair * pair, bytes_accessed=8 * rows * pair, transcendentals=0
        ),
    )(covariance, rotations)


def solution(mesh):
    placed = (P("row", "col"), P(None, "row"))
    return jax.shard_map(
        shards, mesh=mesh, in_specs=placed, out_specs=P("row", "col"), check_vma=False
    )
```

```python
import functools

import jax
import jax.numpy as jnp
from jax import lax
from jax.experimental import pallas as pl
from jax.experimental.pallas import tpu as pltpu
from jax.sharding import PartitionSpec as P

MESH = pl.DeviceIdType.MESH
PLANES = 8
COLUMNS = 8
XS = 4
BF16 = jnp.bfloat16


def row_of(z, hi, k):
    return z * 4 + hi * 2 + k


CHUNKS = 16
SLACK = 2
PARTS = 2
HEAD = 6
EARLY = 6
C_CHUNKS = 8


def kernel(
    c_ref,
    m_ref,
    o_ref,
    c_raw,
    m_raw,
    c_all,
    m_t,
    m_q,
    turned_in,
    t_all,
    y_out,
    hold,
    c_load,
    m_load,
    q_load,
    c_send,
    c_recv,
    e_send,
    e_recv,
    f_send,
    f_recv,
    p_send,
    p_recv,
    v_send,
    v_recv,
    x_send,
    x_recv,
    r_send,
    r_recv,
    g_send,
    g_recv,
    h_send,
    h_recv,
    w_send,
    y_send,
    y_recv,
):
    rows, pair = c_ref.shape
    width = m_ref.shape[1]
    piece = width // 4
    half = pair // 2
    tile = pair // 2

    r = lax.axis_index("row")
    c = lax.axis_index("col")
    z, hi, k = r // 4, r // 2 % 2, r % 2
    x, lo = c // 2, c % 2

    mate = (row_of(z, hi, 1 - k), c)
    twin = (row_of(z, 1 - hi, k), c)
    z_next = (row_of((z + 1) % PLANES, hi, k), c)
    z_prev = (row_of((z + PLANES - 1) % PLANES, hi, k), c)
    across = (row_of(z, 1 - hi, k), x * 2 + 1 - lo)
    x_others = [(r, (x + n) % XS * 2 + lo) for n in range(1, XS)]

    last = COLUMNS - 1

    def column_target(col):
        to = jnp.where(
            hi == 0,
            jnp.where(col == 0, 0, jnp.where(col == last, col, col + 1)),
            jnp.where(col == 0, 1, col - 1),
        )
        upper = jnp.where(col == last, 1, 0)
        return to, jnp.where(hi == 0, upper, jnp.where(col == 0, 0, 1))

    to_col, to_slot = column_target(c)
    src_col = (jnp.where(c <= 1, 0, c - 1), jnp.where(c == last, c, c + 1))
    src_tile = (jnp.where(c == 1, 1, 0), jnp.where(c == last, 0, 1))

    y_z = (
        jnp.where(z == 0, 0, jnp.where(z == PLANES - 1, z, z + 1)),
        jnp.where(z == 0, 1, z - 1),
    )
    y_hi = (jnp.where(z == PLANES - 1, 1, 0), jnp.where(z == 0, 0, 1))
    src_plane = (
        jnp.where(z <= 1, 0, z - 1),
        jnp.where(z == PLANES - 1, z, z + 1),
    )
    src_z = jnp.where(hi == 0, src_plane[0], src_plane[1])
    side_z = jnp.where(hi == 0, src_plane[1], src_plane[0])

    moves_x = to_col // 2 != x

    def own_line(col, h):
        return (hi == 0) & ((col == last - 1) | ((col == 1) & (h == 1)))

    def side_line(col, col_hi, h):
        return (h == 1) & (((col == 2) & (col_hi == 1)) | ((col == last) & (col_hi == 0)))

    def route(b, h):
        own_hi = y_hi[b] == hi
        line = own_line(c, h)
        side = side_line(c, hi, h)
        side_col = jnp.where(c == 2, 3, last - 1)
        leaves = y_z[b] != z
        relayed = jnp.where(own_hi, jnp.where(line, leaves, moves_x), leaves)
        via_hi = jnp.where(own_hi | jnp.logical_not(side), hi, 1 - hi)
        via_x = jnp.where(line, c, x * 2 + to_col % 2)
        via_col = jnp.where(own_hi, via_x, jnp.where(side, side_col, c))
        which = jnp.where(own_hi | side, 1, 0)
        return relayed, which, (row_of(y_z[b], via_hi, k), via_col)

    def final(b, h):
        device = (row_of(y_z[b], y_hi[b], h), to_col)
        return device, (y_z[b] == z) & (y_hi[b] == hi) & (h == k) & (to_col == c)

    peer = x * 2 + 1 - lo
    peer_col, peer_slot = column_target(peer)

    def relay(n, h):
        if n == 0:
            here = (side_z != z) & jnp.logical_not(side_line(c, hi, h))
            return here, (row_of(side_z, hi, k), c), to_col, to_slot
        from_peer = (peer_col // 2 != x) & jnp.logical_not(own_line(peer, h))
        away = src_z != z
        from_own = away & own_line(c, h)
        side_col = jnp.where(c == 3, 2, last)
        from_side = (hi == 0) & (c == 3) | (hi == 1) & (c == last - 1)
        from_side = away & (h == 1) & from_side
        source_hi = jnp.where(from_side, 1 - hi, hi)
        source_col = jnp.where(from_side, side_col, jnp.where(from_own, c, peer))
        end = jnp.where(c == 3, 1, last)
        col = jnp.where(from_side, end, jnp.where(from_own, to_col, peer_col))
        slot = jnp.where(from_side, 1, jnp.where(from_own, to_slot, peer_slot))
        here = from_peer | from_own | from_side
        return here, (row_of(src_z, source_hi, k), source_col), col, slot

    relay_hi = (1 - hi, hi)

    def block_from(slot, core):
        col, source_hi = src_col[slot], src_tile[slot]
        own_hi = source_hi == hi
        line = own_line(col, k)
        side = (source_hi != hi) & side_line(col, source_hi, k)
        away = src_z != z
        relayed = jnp.where(own_hi, jnp.where(line, away, col // 2 != x), away)
        along_x = jnp.where(line, col, col // 2 * 2 + lo)
        via_col = jnp.where(own_hi, along_x, jnp.where(side, jnp.where(col == 2, 3, last - 1), col))
        via_hi = jnp.where(side, hi, source_hi)
        plane = jnp.where(relayed, z, src_z)
        sender_hi = jnp.where(relayed, via_hi, source_hi)
        sender_col = jnp.where(relayed, via_col, col)
        device = (row_of(plane, sender_hi, core), sender_col)
        same = (plane == z) & (sender_hi == hi) & (core == k) & (sender_col == c)
        return device, same

    barrier = pltpu.get_barrier_semaphore()

    def greet(device):
        pl.semaphore_signal(barrier, inc=1, device_id=device, device_id_type=MESH)

    for device in (mate, twin, z_next, z_prev, across, *x_others):
        greet(device)
    expected = jnp.int32(8)
    def greet_if(device, condition):
        @pl.when(condition)
        def _():
            greet(device)

    for n in range(2):
        for h in range(2):
            here, device, _, _ = relay(n, h)
            greet_if(device, here)
            expected = expected + jnp.where(here, 1, 0)
            device, same = block_from(n, h)
            greet_if(device, jnp.logical_not(same))
            sends = route(n, h)[0] | jnp.logical_not(final(n, h)[1])
            expected = expected + jnp.where(sends, 1, 0)

    def remote(src, dst, send, recv, device):
        return pltpu.make_async_remote_copy(
            src_ref=src,
            dst_ref=dst,
            send_sem=send,
            recv_sem=recv,
            device_id=device,
            device_id_type=MESH,
        )

    c_step = rows // C_CHUNKS

    def c_copy(i):
        at = pl.ds(i * c_step, c_step)
        return pltpu.make_async_copy(c_ref.at[at], c_raw.at[at], c_load.at[i])

    up = (z - c + PLANES) % PLANES
    down = (c - z + PLANES) % PLANES
    m_copy = pltpu.make_async_copy(m_ref, m_raw, m_load)
    q_copy = pltpu.make_async_copy(m_ref, m_q, q_load)

    @pl.when(up == 0)
    def _():
        q_copy.start()

    for i in range(C_CHUNKS):
        c_copy(i).start()
    m_copy.start()

    pl.semaphore_wait(barrier, expected)

    def over(part):
        at = pl.ds(part * half, half)
        src = m_ref.at[at, pl.ds(pl.multiple_of(x * piece, piece), piece)]
        return remote(
            src, turned_in.at[at], v_send.at[part], v_recv.at[part], across
        )

    for part in range(2):
        over(part).start()

    def c_rows(of_hi, core, i):
        at = pl.multiple_of(of_hi * tile + core * rows + i * c_step, c_step)
        return c_all.at[pl.ds(at, c_step)]

    def c_mate(i):
        ref = c_rows(hi, k, i)
        return remote(ref, ref, c_send.at[i], c_recv.at[i], mate)

    def c_mate_in(i):
        ref = c_rows(hi, 1 - k, i)
        return remote(ref, ref, c_send.at[i], c_recv.at[i], mate)

    def c_twin(i):
        ref = c_rows(hi, k, i)
        return remote(ref, ref, e_send.at[i], e_recv.at[i], twin)

    def c_twin_in(i):
        ref = c_rows(1 - hi, k, i)
        return remote(ref, ref, e_send.at[i], e_recv.at[i], twin)

    def c_relay(i):
        ref = c_rows(1 - hi, k, i)
        return remote(ref, ref, f_send.at[i], f_recv.at[i], mate)

    def c_relay_in(i):
        ref = c_rows(1 - hi, 1 - k, i)
        return remote(ref, ref, f_send.at[i], f_recv.at[i], mate)

    for i in range(C_CHUNKS):
        c_copy(i).wait()
        at = pl.multiple_of(hi * tile + k * rows + i * c_step, c_step)
        c_all[pl.ds(at, c_step), :] = c_raw[pl.ds(i * c_step, c_step), :].astype(BF16)
        c_mate(i).start()

    @pl.when(up == 0)
    def _():
        q_copy.wait()

    q_step = half // CHUNKS

    def spread(way, n):
        at = pl.multiple_of(way * half + n * q_step, q_step)
        ref = m_q.at[pl.ds(at, q_step)]
        device = (z_next, z_prev)[way]
        return remote(ref, ref, g_send.at[way, n], g_recv.at[way, n], device)

    def pass_on(s):
        for way, distance in ((0, up), (1, down)):
            n = s - SLACK * distance
            here = (n >= 0) & (n < CHUNKS)

            @pl.when(here & (distance > 0))
            def _():
                spread(way, n).wait_recv()

            @pl.when(here & (distance < PLANES - 1))
            def _():
                spread(way, n).start()

    every = 4

    def slots(first, end):
        @pl.loop(first, end)
        def _(s):
            pass_on(s)

            n = s - HEAD

            @pl.when((n >= 0) & (n % every == every - 1) & (n < every * EARLY))
            def _():
                i = n // every
                c_twin_in(i).wait_recv()
                c_relay(i).start()

    slots(0, HEAD)

    m_copy.wait()
    shard = hi * 2 + k
    other = (1 - hi) * 2 + k
    mate_other = (1 - hi) * 2 + 1 - k

    def t_rows(which, quarter):
        return pl.ds(pl.multiple_of(which * width + quarter * piece, piece), piece)

    for quarter in range(4):
        m_t[t_rows(shard, quarter), :] = m_raw[
            :, quarter * piece : (quarter + 1) * piece
        ].T
    own = pl.ds(pl.multiple_of(shard * width, width), width)
    shard_out = remote(m_t.at[own], m_t.at[own], p_send, p_recv, mate)
    shard_out.start()
    mates = pl.ds(pl.multiple_of((hi * 2 + 1 - k) * width, width), width)
    shard_in = remote(m_t.at[mates], m_t.at[mates], p_send, p_recv, mate)

    def along(n, part):
        ref = m_t.at[t_rows(other, x), pl.ds(part * half, half)]
        at = (n - 1, part)
        return remote(ref, ref, x_send.at[at], x_recv.at[at], x_others[n - 1])

    def along_in(n, part):
        quarter = (x + XS - n) % XS
        ref = m_t.at[t_rows(other, quarter), pl.ds(part * half, half)]
        at = (n - 1, part)
        return remote(ref, ref, x_send.at[at], x_recv.at[at], mate)

    def to_mate(n, part, of=other):
        quarter = (x + XS - n) % XS
        ref = m_t.at[t_rows(of, quarter), pl.ds(part * half, half)]
        return remote(ref, ref, r_send.at[n, part], r_recv.at[n, part], mate)

    def turn_over(part):
        at = slice(part * half, (part + 1) * half)
        m_t[t_rows(other, x), at] = turned_in[at, :].T
        for n in range(1, XS):
            along(n, part).start()
        to_mate(0, part).start()

    for part in range(2):
        over(part).wait_recv()
    for i in range(C_CHUNKS):
        c_twin(i).start()
    for part in range(2):
        turn_over(part)
    slots(HEAD, CHUNKS + SLACK * (PLANES - 1))

    def first(start, count):
        step = min(256, count)

        @pl.loop(0, count // step)
        def _(i):
            at = pl.ds(pl.multiple_of(start + i * step, step), step)
            got = jnp.dot(c_all[at, :], m_q[...], preferred_element_type=jnp.float32)
            t_all[at, :] = got.astype(BF16)

    for i in range(C_CHUNKS):
        c_mate_in(i).wait_recv()
    first(hi * tile, tile)
    group = C_CHUNKS // 2
    part_rows = rows // 2
    for n in range(2):
        for i in range(n * group, (n + 1) * group):
            if i >= EARLY:
                c_twin_in(i).wait_recv()
                c_relay(i).start()
        first((1 - hi) * tile + k * rows + n * part_rows, part_rows)
    for n in range(2):
        for i in range(n * group, (n + 1) * group):
            c_relay_in(i).wait_recv()
        first((1 - hi) * tile + (1 - k) * rows + n * part_rows, part_rows)
    for part in range(2):
        for n in range(1, XS):
            along_in(n, part).wait_recv()
            to_mate(n, part).start()
    shard_in.wait_recv()
    for part in range(2):
        for n in range(XS):
            to_mate(n, part, mate_other).wait_recv()

    part_step = width // PARTS

    def place(slot, core):
        at = pl.multiple_of(slot * tile + core * width, width)
        return pl.ds(at, width)

    def y_copies(b, h, part):
        src = y_out.at[pl.ds((b * 2 + h) * width + part * part_step, part_step)]
        at = pl.ds(part * part_step, part_step)
        dst = o_ref.at[at, place(to_slot, k)]
        recv = y_recv.at[to_slot, k, part]
        device, same = final(b, h)
        send = y_send.at[b, h, part]
        straight = remote(src, dst, send, recv, device)
        local = pltpu.make_async_copy(src, dst, recv)
        relayed, n, via = route(b, h)
        held = hold.at[n, pl.ds(h * width + part * part_step, part_step)]
        first_hop = remote(src, held, send, h_recv.at[n, h, part], via)
        return straight, local, first_hop, same, relayed

    def held_in(n, h, part):
        ref = hold.at[n, pl.ds(h * width + part * part_step, part_step)]
        return remote(ref, ref, h_send.at[n, h, part], h_recv.at[n, h, part], mate)

    def second_hop(n, h, part):
        _, _, col, slot = relay(n, h)
        src = hold.at[n, pl.ds(h * width + part * part_step, part_step)]
        dst = o_ref.at[pl.ds(part * part_step, part_step), place(slot, k)]
        device = (row_of(z, relay_hi[n], h), col)
        recv = y_recv.at[slot, k, part]
        return remote(src, dst, w_send.at[n, h, part], recv, device)

    for h in range(2):
        for part in range(PARTS):
            for b in range(2):
                at = pl.ds((b * 2 + h) * width + part * part_step, part_step)
                got = jnp.dot(m_t[at, :], t_all[...], preferred_element_type=jnp.float32)
                y_out[at, :] = got.astype(BF16)
                straight, local, first_hop, same, relayed = y_copies(b, h, part)

                @pl.when(relayed)
                def _():
                    first_hop.start()

                @pl.when(jnp.logical_not(relayed | same))
                def _():
                    straight.start()

                @pl.when(jnp.logical_not(relayed) & same)
                def _():
                    local.start()

    for h in range(2):
        for part in range(PARTS):
            for n in range(2):

                @pl.when(relay(n, h)[0])
                def _():
                    held_in(n, h, part).wait_recv()
                    second_hop(n, h, part).start()

    shard_out.wait_send()
    for i in range(C_CHUNKS):
        c_mate(i).wait_send()
        c_twin(i).wait_send()
        c_relay(i).wait_send()
    for part in range(2):
        over(part).wait_send()
        for n in range(XS):
            to_mate(n, part).wait_send()
        for n in range(1, XS):
            along(n, part).wait_send()

    for way, distance in ((0, up), (1, down)):

        @pl.when(distance < PLANES - 1)
        def _():
            @pl.loop(0, CHUNKS)
            def _(n):
                spread(way, n).wait_send()

    for b in range(2):
        for h in range(2):
            for part in range(PARTS):
                straight, _, _, same, relayed = y_copies(b, h, part)

                @pl.when(relayed | jnp.logical_not(same))
                def _():
                    straight.wait_send()

    for n in range(2):
        for h in range(2):

            @pl.when(relay(n, h)[0])
            def _():
                for part in range(PARTS):
                    second_hop(n, h, part).wait_send()

    for slot in range(2):
        for h in range(2):
            for part in range(PARTS):
                at = pl.ds(part * part_step, part_step)
                ref = o_ref.at[at, pl.ds(slot * tile + h * width, width)]
                recv = y_recv.at[slot, h, part]
                remote(ref, ref, y_send.at[0, 0, 0], recv, mate).wait_recv()


def shards(covariance, rotations):
    rows, pair = covariance.shape
    width = rotations.shape[1]
    dma = pltpu.SemaphoreType.DMA
    return pl.pallas_call(
        kernel,
        out_shape=jax.ShapeDtypeStruct((rows, pair), BF16),
        in_specs=[pl.BlockSpec(memory_space=pl.ANY)] * 2,
        out_specs=pl.BlockSpec(memory_space=pl.ANY),
        scratch_shapes=[
            pltpu.VMEM((rows, pair), jnp.float32),
            pltpu.VMEM((pair, width), BF16),
            pltpu.VMEM((pair, pair), BF16),
            pltpu.VMEM((pair, pair), BF16),
            pltpu.VMEM((pair, width), BF16),
            pltpu.VMEM((pair, width // 4), BF16),
            pltpu.VMEM((pair, width), BF16),
            pltpu.VMEM((pair, width), BF16),
            pltpu.VMEM((2, 2 * width, width), BF16),
            dma((C_CHUNKS,)),
            dma,
            dma,
            dma((C_CHUNKS,)),
            dma((C_CHUNKS,)),
            dma((C_CHUNKS,)),
            dma((C_CHUNKS,)),
            dma((C_CHUNKS,)),
            dma((C_CHUNKS,)),
            dma,
            dma,
            dma((2,)),
            dma((2,)),
            dma((XS - 1, 2)),
            dma((XS - 1, 2)),
            dma((XS, 2)),
            dma((XS, 2)),
            dma((2, CHUNKS)),
            dma((2, CHUNKS)),
            dma((2, 2, PARTS)),
            dma((2, 2, PARTS)),
            dma((2, 2, PARTS)),
            dma((2, 2, PARTS)),
            dma((2, 2, PARTS)),
        ],
        compiler_params=pltpu.CompilerParams(
            collective_id=0,
            has_side_effects=True,
            vmem_limit_bytes=56 * 1024 * 1024,
        ),
        cost_estimate=pl.CostEstimate(
            flops=4 * rows * pair * pair, bytes_accessed=8 * rows * pair, transcendentals=0
        ),
    )(covariance, rotations)


def solution(mesh):
    placed = (P("row", "col"), P(None, "row"))
    return jax.shard_map(
        shards, mesh=mesh, in_specs=placed, out_specs=P("row", "col"), check_vma=False
    )
```

```python
import functools

import jax
import jax.numpy as jnp
from jax import lax
from jax.experimental import pallas as pl
from jax.experimental.pallas import tpu as pltpu
from jax.sharding import PartitionSpec as P

MESH = pl.DeviceIdType.MESH
PLANES = 8
COLUMNS = 8
XS = 4
BF16 = jnp.bfloat16


def row_of(z, hi, k):
    return z * 4 + hi * 2 + k


CHUNKS = 16
SLACK = 2
PARTS = 2
HEAD = 6
EARLY = 6
C_CHUNKS = 8


def kernel(
    c_ref,
    m_ref,
    o_ref,
    c_raw,
    m_raw,
    c_all,
    m_t,
    m_q,
    turned_in,
    t_all,
    y_out,
    hold,
    c_load,
    m_load,
    q_load,
    c_send,
    c_recv,
    e_send,
    e_recv,
    f_send,
    f_recv,
    p_send,
    p_recv,
    v_send,
    v_recv,
    x_send,
    x_recv,
    r_send,
    r_recv,
    g_send,
    g_recv,
    h_send,
    h_recv,
    w_send,
    y_send,
    y_recv,
):
    rows, pair = c_ref.shape
    width = m_ref.shape[1]
    piece = width // 4
    half = pair // 2
    tile = pair // 2

    r = lax.axis_index("row")
    c = lax.axis_index("col")
    z, hi, k = r // 4, r // 2 % 2, r % 2
    x, lo = c // 2, c % 2

    mate = (row_of(z, hi, 1 - k), c)
    twin = (row_of(z, 1 - hi, k), c)
    z_next = (row_of((z + 1) % PLANES, hi, k), c)
    z_prev = (row_of((z + PLANES - 1) % PLANES, hi, k), c)
    across = (row_of(z, 1 - hi, k), x * 2 + 1 - lo)
    x_others = [(r, (x + n) % XS * 2 + lo) for n in range(1, XS)]

    last = COLUMNS - 1

    def column_target(col):
        to = jnp.where(
            hi == 0,
            jnp.where(col == 0, 0, jnp.where(col == last, col, col + 1)),
            jnp.where(col == 0, 1, col - 1),
        )
        upper = jnp.where(col == last, 1, 0)
        return to, jnp.where(hi == 0, upper, jnp.where(col == 0, 0, 1))

    to_col, to_slot = column_target(c)
    src_col = (jnp.where(c <= 1, 0, c - 1), jnp.where(c == last, c, c + 1))
    src_tile = (jnp.where(c == 1, 1, 0), jnp.where(c == last, 0, 1))

    y_z = (
        jnp.where(z == 0, 0, jnp.where(z == PLANES - 1, z, z + 1)),
        jnp.where(z == 0, 1, z - 1),
    )
    y_hi = (jnp.where(z == PLANES - 1, 1, 0), jnp.where(z == 0, 0, 1))
    src_plane = (
        jnp.where(z <= 1, 0, z - 1),
        jnp.where(z == PLANES - 1, z, z + 1),
    )
    src_z = jnp.where(hi == 0, src_plane[0], src_plane[1])
    side_z = jnp.where(hi == 0, src_plane[1], src_plane[0])

    moves_x = to_col // 2 != x

    def own_line(col, h):
        return (hi == 0) & ((col == last - 1) | ((col == 1) & (h == 1)))

    def side_line(col, col_hi, h):
        return (h == 1) & (((col == 2) & (col_hi == 1)) | ((col == last) & (col_hi == 0)))

    def route(b, h):
        own_hi = y_hi[b] == hi
        line = own_line(c, h)
        side = side_line(c, hi, h)
        side_col = jnp.where(c == 2, 3, last - 1)
        leaves = y_z[b] != z
        relayed = jnp.where(own_hi, jnp.where(line, leaves, moves_x), leaves | side)
        via_hi = jnp.where(own_hi | jnp.logical_not(side), hi, 1 - hi)
        via_x = jnp.where(line, c, x * 2 + to_col % 2)
        via_col = jnp.where(own_hi, via_x, jnp.where(side, side_col, c))
        which = jnp.where(own_hi | side, 1, 0)
        return relayed, which, (row_of(y_z[b], via_hi, k), via_col)

    def final(b, h):
        device = (row_of(y_z[b], y_hi[b], h), to_col)
        return device, (y_z[b] == z) & (y_hi[b] == hi) & (h == k) & (to_col == c)

    peer = x * 2 + 1 - lo
    peer_col, peer_slot = column_target(peer)

    def relay(n, h):
        if n == 0:
            here = (side_z != z) & jnp.logical_not(side_line(c, hi, h))
            return here, (row_of(side_z, hi, k), c), to_col, to_slot
        from_peer = (peer_col // 2 != x) & jnp.logical_not(own_line(peer, h))
        away = src_z != z
        from_own = away & own_line(c, h)
        side_col = jnp.where(c == 3, 2, last)
        from_side = (hi == 0) & (c == 3) | (hi == 1) & (c == last - 1)
        from_side = (h == 1) & from_side
        source_hi = jnp.where(from_side, 1 - hi, hi)
        source_col = jnp.where(from_side, side_col, jnp.where(from_own, c, peer))
        end = jnp.where(c == 3, 1, last)
        col = jnp.where(from_side, end, jnp.where(from_own, to_col, peer_col))
        slot = jnp.where(from_side, 1, jnp.where(from_own, to_slot, peer_slot))
        here = from_peer | from_own | from_side
        return here, (row_of(src_z, source_hi, k), source_col), col, slot

    relay_hi = (1 - hi, hi)

    def block_from(slot, core):
        col, source_hi = src_col[slot], src_tile[slot]
        own_hi = source_hi == hi
        line = own_line(col, k)
        side = (source_hi != hi) & side_line(col, source_hi, k)
        away = src_z != z
        relayed = jnp.where(own_hi, jnp.where(line, away, col // 2 != x), away | side)
        along_x = jnp.where(line, col, col // 2 * 2 + lo)
        via_col = jnp.where(own_hi, along_x, jnp.where(side, jnp.where(col == 2, 3, last - 1), col))
        via_hi = jnp.where(side, hi, source_hi)
        plane = jnp.where(relayed, z, src_z)
        sender_hi = jnp.where(relayed, via_hi, source_hi)
        sender_col = jnp.where(relayed, via_col, col)
        device = (row_of(plane, sender_hi, core), sender_col)
        same = (plane == z) & (sender_hi == hi) & (core == k) & (sender_col == c)
        return device, same

    barrier = pltpu.get_barrier_semaphore()

    def greet(device):
        pl.semaphore_signal(barrier, inc=1, device_id=device, device_id_type=MESH)

    for device in (mate, twin, z_next, z_prev, across, *x_others):
        greet(device)
    expected = jnp.int32(8)
    def greet_if(device, condition):
        @pl.when(condition)
        def _():
            greet(device)

    for n in range(2):
        for h in range(2):
            here, device, _, _ = relay(n, h)
            greet_if(device, here)
            expected = expected + jnp.where(here, 1, 0)
            device, same = block_from(n, h)
            greet_if(device, jnp.logical_not(same))
            sends = route(n, h)[0] | jnp.logical_not(final(n, h)[1])
            expected = expected + jnp.where(sends, 1, 0)

    def remote(src, dst, send, recv, device):
        return pltpu.make_async_remote_copy(
            src_ref=src,
            dst_ref=dst,
            send_sem=send,
            recv_sem=recv,
            device_id=device,
            device_id_type=MESH,
        )

    c_step = rows // C_CHUNKS

    def c_copy(i):
        at = pl.ds(i * c_step, c_step)
        return pltpu.make_async_copy(c_ref.at[at], c_raw.at[at], c_load.at[i])

    up = (z - c + PLANES) % PLANES
    down = (c - z + PLANES) % PLANES
    m_copy = pltpu.make_async_copy(m_ref, m_raw, m_load)
    q_copy = pltpu.make_async_copy(m_ref, m_q, q_load)

    @pl.when(up == 0)
    def _():
        q_copy.start()

    for i in range(C_CHUNKS):
        c_copy(i).start()
    m_copy.start()

    pl.semaphore_wait(barrier, expected)

    def over(part):
        at = pl.ds(part * half, half)
        src = m_ref.at[at, pl.ds(pl.multiple_of(x * piece, piece), piece)]
        return remote(
            src, turned_in.at[at], v_send.at[part], v_recv.at[part], across
        )

    for part in range(2):
        over(part).start()

    def c_rows(of_hi, core, i):
        at = pl.multiple_of(of_hi * tile + core * rows + i * c_step, c_step)
        return c_all.at[pl.ds(at, c_step)]

    def c_mate(i):
        ref = c_rows(hi, k, i)
        return remote(ref, ref, c_send.at[i], c_recv.at[i], mate)

    def c_mate_in(i):
        ref = c_rows(hi, 1 - k, i)
        return remote(ref, ref, c_send.at[i], c_recv.at[i], mate)

    def c_twin(i):
        ref = c_rows(hi, k, i)
        return remote(ref, ref, e_send.at[i], e_recv.at[i], twin)

    def c_twin_in(i):
        ref = c_rows(1 - hi, k, i)
        return remote(ref, ref, e_send.at[i], e_recv.at[i], twin)

    def c_relay(i):
        ref = c_rows(1 - hi, k, i)
        return remote(ref, ref, f_send.at[i], f_recv.at[i], mate)

    def c_relay_in(i):
        ref = c_rows(1 - hi, 1 - k, i)
        return remote(ref, ref, f_send.at[i], f_recv.at[i], mate)

    for i in range(C_CHUNKS):
        c_copy(i).wait()
        at = pl.multiple_of(hi * tile + k * rows + i * c_step, c_step)
        c_all[pl.ds(at, c_step), :] = c_raw[pl.ds(i * c_step, c_step), :].astype(BF16)
        c_mate(i).start()

    @pl.when(up == 0)
    def _():
        q_copy.wait()

    q_step = half // CHUNKS

    def spread(way, n):
        at = pl.multiple_of(way * half + n * q_step, q_step)
        ref = m_q.at[pl.ds(at, q_step)]
        device = (z_next, z_prev)[way]
        return remote(ref, ref, g_send.at[way, n], g_recv.at[way, n], device)

    def pass_on(s):
        for way, distance in ((0, up), (1, down)):
            n = s - SLACK * distance
            here = (n >= 0) & (n < CHUNKS)

            @pl.when(here & (distance > 0))
            def _():
                spread(way, n).wait_recv()

            @pl.when(here & (distance < PLANES - 1))
            def _():
                spread(way, n).start()

    every = 4

    def slots(first, end):
        @pl.loop(first, end)
        def _(s):
            pass_on(s)

            n = s - HEAD

            @pl.when((n >= 0) & (n % every == every - 1) & (n < every * EARLY))
            def _():
                i = n // every
                c_twin_in(i).wait_recv()
                c_relay(i).start()

    slots(0, HEAD)

    m_copy.wait()
    shard = hi * 2 + k
    other = (1 - hi) * 2 + k
    mate_other = (1 - hi) * 2 + 1 - k

    def t_rows(which, quarter):
        return pl.ds(pl.multiple_of(which * width + quarter * piece, piece), piece)

    for quarter in range(4):
        m_t[t_rows(shard, quarter), :] = m_raw[
            :, quarter * piece : (quarter + 1) * piece
        ].T
    own = pl.ds(pl.multiple_of(shard * width, width), width)
    shard_out = remote(m_t.at[own], m_t.at[own], p_send, p_recv, mate)
    shard_out.start()
    mates = pl.ds(pl.multiple_of((hi * 2 + 1 - k) * width, width), width)
    shard_in = remote(m_t.at[mates], m_t.at[mates], p_send, p_recv, mate)

    def along(n, part):
        ref = m_t.at[t_rows(other, x), pl.ds(part * half, half)]
        at = (n - 1, part)
        return remote(ref, ref, x_send.at[at], x_recv.at[at], x_others[n - 1])

    def along_in(n, part):
        quarter = (x + XS - n) % XS
        ref = m_t.at[t_rows(other, quarter), pl.ds(part * half, half)]
        at = (n - 1, part)
        return remote(ref, ref, x_send.at[at], x_recv.at[at], mate)

    def to_mate(n, part, of=other):
        quarter = (x + XS - n) % XS
        ref = m_t.at[t_rows(of, quarter), pl.ds(part * half, half)]
        return remote(ref, ref, r_send.at[n, part], r_recv.at[n, part], mate)

    def turn_over(part):
        at = slice(part * half, (part + 1) * half)
        m_t[t_rows(other, x), at] = turned_in[at, :].T
        for n in range(1, XS):
            along(n, part).start()
        to_mate(0, part).start()

    for part in range(2):
        over(part).wait_recv()
    for i in range(C_CHUNKS):
        c_twin(i).start()
    for part in range(2):
        turn_over(part)
    slots(HEAD, CHUNKS + SLACK * (PLANES - 1))

    def first(start, count):
        step = min(256, count)

        @pl.loop(0, count // step)
        def _(i):
            at = pl.ds(pl.multiple_of(start + i * step, step), step)
            got = jnp.dot(c_all[at, :], m_q[...], preferred_element_type=jnp.float32)
            t_all[at, :] = got.astype(BF16)

    for i in range(C_CHUNKS):
        c_mate_in(i).wait_recv()
    first(hi * tile, tile)
    group = C_CHUNKS // 2
    part_rows = rows // 2
    for n in range(2):
        for i in range(n * group, (n + 1) * group):
            if i >= EARLY:
                c_twin_in(i).wait_recv()
                c_relay(i).start()
        first((1 - hi) * tile + k * rows + n * part_rows, part_rows)
    for n in range(2):
        for i in range(n * group, (n + 1) * group):
            c_relay_in(i).wait_recv()
        first((1 - hi) * tile + (1 - k) * rows + n * part_rows, part_rows)
    for part in range(2):
        for n in range(1, XS):
            along_in(n, part).wait_recv()
            to_mate(n, part).start()
    shard_in.wait_recv()
    for part in range(2):
        for n in range(XS):
            to_mate(n, part, mate_other).wait_recv()

    part_step = width // PARTS

    def place(slot, core):
        at = pl.multiple_of(slot * tile + core * width, width)
        return pl.ds(at, width)

    def y_copies(b, h, part):
        src = y_out.at[pl.ds((b * 2 + h) * width + part * part_step, part_step)]
        at = pl.ds(part * part_step, part_step)
        dst = o_ref.at[at, place(to_slot, k)]
        recv = y_recv.at[to_slot, k, part]
        device, same = final(b, h)
        send = y_send.at[b, h, part]
        straight = remote(src, dst, send, recv, device)
        local = pltpu.make_async_copy(src, dst, recv)
        relayed, n, via = route(b, h)
        held = hold.at[n, pl.ds(h * width + part * part_step, part_step)]
        first_hop = remote(src, held, send, h_recv.at[n, h, part], via)
        return straight, local, first_hop, same, relayed

    def held_in(n, h, part):
        ref = hold.at[n, pl.ds(h * width + part * part_step, part_step)]
        return remote(ref, ref, h_send.at[n, h, part], h_recv.at[n, h, part], mate)

    def second_hop(n, h, part):
        _, _, col, slot = relay(n, h)
        src = hold.at[n, pl.ds(h * width + part * part_step, part_step)]
        dst = o_ref.at[pl.ds(part * part_step, part_step), place(slot, k)]
        device = (row_of(z, relay_hi[n], h), col)
        recv = y_recv.at[slot, k, part]
        return remote(src, dst, w_send.at[n, h, part], recv, device)

    for h in range(2):
        for part in range(PARTS):
            for b in range(2):
                at = pl.ds((b * 2 + h) * width + part * part_step, part_step)
                got = jnp.dot(m_t[at, :], t_all[...], preferred_element_type=jnp.float32)
                y_out[at, :] = got.astype(BF16)
                straight, local, first_hop, same, relayed = y_copies(b, h, part)

                @pl.when(relayed)
                def _():
                    first_hop.start()

                @pl.when(jnp.logical_not(relayed | same))
                def _():
                    straight.start()

                @pl.when(jnp.logical_not(relayed) & same)
                def _():
                    local.start()

    for h in range(2):
        for part in range(PARTS):
            for n in range(2):

                @pl.when(relay(n, h)[0])
                def _():
                    held_in(n, h, part).wait_recv()
                    second_hop(n, h, part).start()

    shard_out.wait_send()
    for i in range(C_CHUNKS):
        c_mate(i).wait_send()
        c_twin(i).wait_send()
        c_relay(i).wait_send()
    for part in range(2):
        over(part).wait_send()
        for n in range(XS):
            to_mate(n, part).wait_send()
        for n in range(1, XS):
            along(n, part).wait_send()

    for way, distance in ((0, up), (1, down)):

        @pl.when(distance < PLANES - 1)
        def _():
            @pl.loop(0, CHUNKS)
            def _(n):
                spread(way, n).wait_send()

    for b in range(2):
        for h in range(2):
            for part in range(PARTS):
                straight, _, _, same, relayed = y_copies(b, h, part)

                @pl.when(relayed | jnp.logical_not(same))
                def _():
                    straight.wait_send()

    for n in range(2):
        for h in range(2):

            @pl.when(relay(n, h)[0])
            def _():
                for part in range(PARTS):
                    second_hop(n, h, part).wait_send()

    for slot in range(2):
        for h in range(2):
            for part in range(PARTS):
                at = pl.ds(part * part_step, part_step)
                ref = o_ref.at[at, pl.ds(slot * tile + h * width, width)]
                recv = y_recv.at[slot, h, part]
                remote(ref, ref, y_send.at[0, 0, 0], recv, mate).wait_recv()


def shards(covariance, rotations):
    rows, pair = covariance.shape
    width = rotations.shape[1]
    dma = pltpu.SemaphoreType.DMA
    return pl.pallas_call(
        kernel,
        out_shape=jax.ShapeDtypeStruct((rows, pair), BF16),
        in_specs=[pl.BlockSpec(memory_space=pl.ANY)] * 2,
        out_specs=pl.BlockSpec(memory_space=pl.ANY),
        scratch_shapes=[
            pltpu.VMEM((rows, pair), jnp.float32),
            pltpu.VMEM((pair, width), BF16),
            pltpu.VMEM((pair, pair), BF16),
            pltpu.VMEM((pair, pair), BF16),
            pltpu.VMEM((pair, width), BF16),
            pltpu.VMEM((pair, width // 4), BF16),
            pltpu.VMEM((pair, width), BF16),
            pltpu.VMEM((pair, width), BF16),
            pltpu.VMEM((2, 2 * width, width), BF16),
            dma((C_CHUNKS,)),
            dma,
            dma,
            dma((C_CHUNKS,)),
            dma((C_CHUNKS,)),
            dma((C_CHUNKS,)),
            dma((C_CHUNKS,)),
            dma((C_CHUNKS,)),
            dma((C_CHUNKS,)),
            dma,
            dma,
            dma((2,)),
            dma((2,)),
            dma((XS - 1, 2)),
            dma((XS - 1, 2)),
            dma((XS, 2)),
            dma((XS, 2)),
            dma((2, CHUNKS)),
            dma((2, CHUNKS)),
            dma((2, 2, PARTS)),
            dma((2, 2, PARTS)),
            dma((2, 2, PARTS)),
            dma((2, 2, PARTS)),
            dma((2, 2, PARTS)),
        ],
        compiler_params=pltpu.CompilerParams(
            collective_id=0,
            has_side_effects=True,
            vmem_limit_bytes=56 * 1024 * 1024,
        ),
        cost_estimate=pl.CostEstimate(
            flops=4 * rows * pair * pair, bytes_accessed=8 * rows * pair, transcendentals=0
        ),
    )(covariance, rotations)


def solution(mesh):
    placed = (P("row", "col"), P(None, "row"))
    return jax.shard_map(
        shards, mesh=mesh, in_specs=placed, out_specs=P("row", "col"), check_vma=False
    )
```

```python
import functools

import jax
import jax.numpy as jnp
from jax import lax
from jax.experimental import pallas as pl
from jax.experimental.pallas import tpu as pltpu
from jax.sharding import PartitionSpec as P

MESH = pl.DeviceIdType.MESH
PLANES = 8
COLUMNS = 8
XS = 4
BF16 = jnp.bfloat16


def row_of(z, hi, k):
    return z * 4 + hi * 2 + k


CHUNKS = 8
SLACK = 2
PARTS = 2
HEAD = 6
EARLY = 4
C_CHUNKS = 8


def kernel(
    c_ref,
    m_ref,
    o_ref,
    c_raw,
    m_raw,
    c_all,
    m_t,
    m_q,
    turned_in,
    t_all,
    y_out,
    hold,
    c_load,
    m_load,
    q_load,
    c_send,
    c_recv,
    e_send,
    e_recv,
    f_send,
    f_recv,
    p_send,
    p_recv,
    v_send,
    v_recv,
    x_send,
    x_recv,
    r_send,
    r_recv,
    g_send,
    g_recv,
    h_send,
    h_recv,
    w_send,
    y_send,
    y_recv,
):
    rows, pair = c_ref.shape
    width = m_ref.shape[1]
    piece = width // 4
    half = pair // 2
    tile = pair // 2

    r = lax.axis_index("row")
    c = lax.axis_index("col")
    z, hi, k = r // 4, r // 2 % 2, r % 2
    x, lo = c // 2, c % 2

    mate = (row_of(z, hi, 1 - k), c)
    twin = (row_of(z, 1 - hi, k), c)
    z_next = (row_of((z + 1) % PLANES, hi, k), c)
    z_prev = (row_of((z + PLANES - 1) % PLANES, hi, k), c)
    across = (row_of(z, 1 - hi, k), x * 2 + 1 - lo)
    x_others = [(r, (x + n) % XS * 2 + lo) for n in range(1, XS)]

    last = COLUMNS - 1

    def column_target(col):
        to = jnp.where(
            hi == 0,
            jnp.where(col == 0, 0, jnp.where(col == last, col, col + 1)),
            jnp.where(col == 0, 1, col - 1),
        )
        upper = jnp.where(col == last, 1, 0)
        return to, jnp.where(hi == 0, upper, jnp.where(col == 0, 0, 1))

    to_col, to_slot = column_target(c)
    src_col = (jnp.where(c <= 1, 0, c - 1), jnp.where(c == last, c, c + 1))
    src_tile = (jnp.where(c == 1, 1, 0), jnp.where(c == last, 0, 1))

    y_z = (
        jnp.where(z == 0, 0, jnp.where(z == PLANES - 1, z, z + 1)),
        jnp.where(z == 0, 1, z - 1),
    )
    y_hi = (jnp.where(z == PLANES - 1, 1, 0), jnp.where(z == 0, 0, 1))
    src_plane = (
        jnp.where(z <= 1, 0, z - 1),
        jnp.where(z == PLANES - 1, z, z + 1),
    )
    src_z = jnp.where(hi == 0, src_plane[0], src_plane[1])
    side_z = jnp.where(hi == 0, src_plane[1], src_plane[0])

    moves_x = to_col // 2 != x

    def own_line(col, h):
        return (hi == 0) & ((col == last - 1) | ((col == 1) & (h == 1)))

    def side_line(col, col_hi, h):
        return (h == 1) & (((col == 2) & (col_hi == 1)) | ((col == last) & (col_hi == 0)))

    def route(b, h):
        own_hi = y_hi[b] == hi
        line = own_line(c, h)
        side = side_line(c, hi, h)
        side_col = jnp.where(c == 2, 3, last - 1)
        leaves = y_z[b] != z
        relayed = jnp.where(own_hi, jnp.where(line, leaves, moves_x), leaves | side)
        via_hi = jnp.where(own_hi | jnp.logical_not(side), hi, 1 - hi)
        via_x = jnp.where(line, c, x * 2 + to_col % 2)
        via_col = jnp.where(own_hi, via_x, jnp.where(side, side_col, c))
        which = jnp.where(own_hi | side, 1, 0)
        return relayed, which, (row_of(y_z[b], via_hi, k), via_col)

    def final(b, h):
        device = (row_of(y_z[b], y_hi[b], h), to_col)
        return device, (y_z[b] == z) & (y_hi[b] == hi) & (h == k) & (to_col == c)

    peer = x * 2 + 1 - lo
    peer_col, peer_slot = column_target(peer)

    def relay(n, h):
        if n == 0:
            here = (side_z != z) & jnp.logical_not(side_line(c, hi, h))
            return here, (row_of(side_z, hi, k), c), to_col, to_slot
        from_peer = (peer_col // 2 != x) & jnp.logical_not(own_line(peer, h))
        away = src_z != z
        from_own = away & own_line(c, h)
        side_col = jnp.where(c == 3, 2, last)
        from_side = (hi == 0) & (c == 3) | (hi == 1) & (c == last - 1)
        from_side = (h == 1) & from_side
        source_hi = jnp.where(from_side, 1 - hi, hi)
        source_col = jnp.where(from_side, side_col, jnp.where(from_own, c, peer))
        end = jnp.where(c == 3, 1, last)
        col = jnp.where(from_side, end, jnp.where(from_own, to_col, peer_col))
        slot = jnp.where(from_side, 1, jnp.where(from_own, to_slot, peer_slot))
        here = from_peer | from_own | from_side
        return here, (row_of(src_z, source_hi, k), source_col), col, slot

    relay_hi = (1 - hi, hi)

    def block_from(slot, core):
        col, source_hi = src_col[slot], src_tile[slot]
        own_hi = source_hi == hi
        line = own_line(col, k)
        side = (source_hi != hi) & side_line(col, source_hi, k)
        away = src_z != z
        relayed = jnp.where(own_hi, jnp.where(line, away, col // 2 != x), away | side)
        along_x = jnp.where(line, col, col // 2 * 2 + lo)
        via_col = jnp.where(own_hi, along_x, jnp.where(side, jnp.where(col == 2, 3, last - 1), col))
        via_hi = jnp.where(side, hi, source_hi)
        plane = jnp.where(relayed, z, src_z)
        sender_hi = jnp.where(relayed, via_hi, source_hi)
        sender_col = jnp.where(relayed, via_col, col)
        device = (row_of(plane, sender_hi, core), sender_col)
        same = (plane == z) & (sender_hi == hi) & (core == k) & (sender_col == c)
        return device, same

    barrier = pltpu.get_barrier_semaphore()

    def greet(device):
        pl.semaphore_signal(barrier, inc=1, device_id=device, device_id_type=MESH)

    for device in (mate, twin, z_next, z_prev, across, *x_others):
        greet(device)
    expected = jnp.int32(8)
    def greet_if(device, condition):
        @pl.when(condition)
        def _():
            greet(device)

    for n in range(2):
        for h in range(2):
            here, device, _, _ = relay(n, h)
            greet_if(device, here)
            expected = expected + jnp.where(here, 1, 0)
            device, same = block_from(n, h)
            greet_if(device, jnp.logical_not(same))
            sends = route(n, h)[0] | jnp.logical_not(final(n, h)[1])
            expected = expected + jnp.where(sends, 1, 0)

    def remote(src, dst, send, recv, device):
        return pltpu.make_async_remote_copy(
            src_ref=src,
            dst_ref=dst,
            send_sem=send,
            recv_sem=recv,
            device_id=device,
            device_id_type=MESH,
        )

    c_step = rows // C_CHUNKS

    def c_copy(i):
        at = pl.ds(i * c_step, c_step)
        return pltpu.make_async_copy(c_ref.at[at], c_raw.at[at], c_load.at[i])

    up = (z - c + PLANES) % PLANES
    down = (c - z + PLANES) % PLANES
    m_copy = pltpu.make_async_copy(m_ref, m_raw, m_load)
    q_copy = pltpu.make_async_copy(m_ref, m_q, q_load)

    @pl.when(up == 0)
    def _():
        q_copy.start()

    for i in range(C_CHUNKS):
        c_copy(i).start()
    m_copy.start()

    pl.semaphore_wait(barrier, expected)

    def over(part):
        at = pl.ds(part * half, half)
        src = m_ref.at[at, pl.ds(pl.multiple_of(x * piece, piece), piece)]
        return remote(
            src, turned_in.at[at], v_send.at[part], v_recv.at[part], across
        )

    for part in range(2):
        over(part).start()

    def c_rows(of_hi, core, i):
        at = pl.multiple_of(of_hi * tile + core * rows + i * c_step, c_step)
        return c_all.at[pl.ds(at, c_step)]

    def c_mate(i):
        ref = c_rows(hi, k, i)
        return remote(ref, ref, c_send.at[i], c_recv.at[i], mate)

    def c_mate_in(i):
        ref = c_rows(hi, 1 - k, i)
        return remote(ref, ref, c_send.at[i], c_recv.at[i], mate)

    def c_twin(i):
        ref = c_rows(hi, k, i)
        return remote(ref, ref, e_send.at[i], e_recv.at[i], twin)

    def c_twin_in(i):
        ref = c_rows(1 - hi, k, i)
        return remote(ref, ref, e_send.at[i], e_recv.at[i], twin)

    def c_relay(i):
        ref = c_rows(1 - hi, k, i)
        return remote(ref, ref, f_send.at[i], f_recv.at[i], mate)

    def c_relay_in(i):
        ref = c_rows(1 - hi, 1 - k, i)
        return remote(ref, ref, f_send.at[i], f_recv.at[i], mate)

    for i in range(C_CHUNKS):
        c_copy(i).wait()
        at = pl.multiple_of(hi * tile + k * rows + i * c_step, c_step)
        c_all[pl.ds(at, c_step), :] = c_raw[pl.ds(i * c_step, c_step), :].astype(BF16)
        c_mate(i).start()

    @pl.when(up == 0)
    def _():
        q_copy.wait()

    q_step = half // CHUNKS

    def spread(way, n):
        at = pl.multiple_of(way * half + n * q_step, q_step)
        ref = m_q.at[pl.ds(at, q_step)]
        device = (z_next, z_prev)[way]
        return remote(ref, ref, g_send.at[way, n], g_recv.at[way, n], device)

    def pass_on(s):
        for way, distance in ((0, up), (1, down)):
            n = s - SLACK * distance
            here = (n >= 0) & (n < CHUNKS)

            @pl.when(here & (distance > 0))
            def _():
                spread(way, n).wait_recv()

            @pl.when(here & (distance < PLANES - 1))
            def _():
                spread(way, n).start()

    every = 4

    def slots(first, end):
        @pl.loop(first, end)
        def _(s):
            pass_on(s)

            n = s - HEAD

            @pl.when((n >= 0) & (n % every == every - 1) & (n < every * EARLY))
            def _():
                i = n // every
                c_twin_in(i).wait_recv()
                c_relay(i).start()

    slots(0, HEAD)

    m_copy.wait()
    shard = hi * 2 + k
    other = (1 - hi) * 2 + k
    mate_other = (1 - hi) * 2 + 1 - k

    def t_rows(which, quarter):
        return pl.ds(pl.multiple_of(which * width + quarter * piece, piece), piece)

    for quarter in range(4):
        m_t[t_rows(shard, quarter), :] = m_raw[
            :, quarter * piece : (quarter + 1) * piece
        ].T
    own = pl.ds(pl.multiple_of(shard * width, width), width)
    shard_out = remote(m_t.at[own], m_t.at[own], p_send, p_recv, mate)
    shard_out.start()
    mates = pl.ds(pl.multiple_of((hi * 2 + 1 - k) * width, width), width)
    shard_in = remote(m_t.at[mates], m_t.at[mates], p_send, p_recv, mate)

    def along(n, part):
        ref = m_t.at[t_rows(other, x), pl.ds(part * half, half)]
        at = (n - 1, part)
        return remote(ref, ref, x_send.at[at], x_recv.at[at], x_others[n - 1])

    def along_in(n, part):
        quarter = (x + XS - n) % XS
        ref = m_t.at[t_rows(other, quarter), pl.ds(part * half, half)]
        at = (n - 1, part)
        return remote(ref, ref, x_send.at[at], x_recv.at[at], mate)

    def to_mate(n, part, of=other):
        quarter = (x + XS - n) % XS
        ref = m_t.at[t_rows(of, quarter), pl.ds(part * half, half)]
        return remote(ref, ref, r_send.at[n, part], r_recv.at[n, part], mate)

    def turn_over(part):
        at = slice(part * half, (part + 1) * half)
        m_t[t_rows(other, x), at] = turned_in[at, :].T
        for n in range(1, XS):
            along(n, part).start()
        to_mate(0, part).start()

    for part in range(2):
        over(part).wait_recv()
    for i in range(C_CHUNKS):
        c_twin(i).start()
    for part in range(2):
        turn_over(part)
    slots(HEAD, CHUNKS + SLACK * (PLANES - 1))

    def first(start, count):
        step = min(256, count)

        @pl.loop(0, count // step)
        def _(i):
            at = pl.ds(pl.multiple_of(start + i * step, step), step)
            got = jnp.dot(c_all[at, :], m_q[...], preferred_element_type=jnp.float32)
            t_all[at, :] = got.astype(BF16)

    for i in range(C_CHUNKS):
        c_mate_in(i).wait_recv()
    first(hi * tile, tile)
    group = C_CHUNKS // 2
    part_rows = rows // 2
    for n in range(2):
        for i in range(n * group, (n + 1) * group):
            if i >= EARLY:
                c_twin_in(i).wait_recv()
                c_relay(i).start()
        first((1 - hi) * tile + k * rows + n * part_rows, part_rows)
    for n in range(2):
        for i in range(n * group, (n + 1) * group):
            c_relay_in(i).wait_recv()
        first((1 - hi) * tile + (1 - k) * rows + n * part_rows, part_rows)
    for part in range(2):
        for n in range(1, XS):
            along_in(n, part).wait_recv()
            to_mate(n, part).start()
    shard_in.wait_recv()
    for part in range(2):
        for n in range(XS):
            to_mate(n, part, mate_other).wait_recv()

    part_step = width // PARTS

    def place(slot, core):
        at = pl.multiple_of(slot * tile + core * width, width)
        return pl.ds(at, width)

    def y_copies(b, h, part):
        src = y_out.at[pl.ds((b * 2 + h) * width + part * part_step, part_step)]
        at = pl.ds(part * part_step, part_step)
        dst = o_ref.at[at, place(to_slot, k)]
        recv = y_recv.at[to_slot, k, part]
        device, same = final(b, h)
        send = y_send.at[b, h, part]
        straight = remote(src, dst, send, recv, device)
        local = pltpu.make_async_copy(src, dst, recv)
        relayed, n, via = route(b, h)
        held = hold.at[n, pl.ds(h * width + part * part_step, part_step)]
        first_hop = remote(src, held, send, h_recv.at[n, h, part], via)
        return straight, local, first_hop, same, relayed

    def held_in(n, h, part):
        ref = hold.at[n, pl.ds(h * width + part * part_step, part_step)]
        return remote(ref, ref, h_send.at[n, h, part], h_recv.at[n, h, part], mate)

    def second_hop(n, h, part):
        _, _, col, slot = relay(n, h)
        src = hold.at[n, pl.ds(h * width + part * part_step, part_step)]
        dst = o_ref.at[pl.ds(part * part_step, part_step), place(slot, k)]
        device = (row_of(z, relay_hi[n], h), col)
        recv = y_recv.at[slot, k, part]
        return remote(src, dst, w_send.at[n, h, part], recv, device)

    for h in range(2):
        for part in range(PARTS):
            for b in range(2):
                at = pl.ds((b * 2 + h) * width + part * part_step, part_step)
                got = jnp.dot(m_t[at, :], t_all[...], preferred_element_type=jnp.float32)
                y_out[at, :] = got.astype(BF16)
                straight, local, first_hop, same, relayed = y_copies(b, h, part)

                @pl.when(relayed)
                def _():
                    first_hop.start()

                @pl.when(jnp.logical_not(relayed | same))
                def _():
                    straight.start()

                @pl.when(jnp.logical_not(relayed) & same)
                def _():
                    local.start()

    for h in range(2):
        for part in range(PARTS):
            for n in range(2):

                @pl.when(relay(n, h)[0])
                def _():
                    held_in(n, h, part).wait_recv()
                    second_hop(n, h, part).start()

    shard_out.wait_send()
    for i in range(C_CHUNKS):
        c_mate(i).wait_send()
        c_twin(i).wait_send()
        c_relay(i).wait_send()
    for part in range(2):
        over(part).wait_send()
        for n in range(XS):
            to_mate(n, part).wait_send()
        for n in range(1, XS):
            along(n, part).wait_send()

    for way, distance in ((0, up), (1, down)):

        @pl.when(distance < PLANES - 1)
        def _():
            @pl.loop(0, CHUNKS)
            def _(n):
                spread(way, n).wait_send()

    for b in range(2):
        for h in range(2):
            for part in range(PARTS):
                straight, _, _, same, relayed = y_copies(b, h, part)

                @pl.when(relayed | jnp.logical_not(same))
                def _():
                    straight.wait_send()

    for n in range(2):
        for h in range(2):

            @pl.when(relay(n, h)[0])
            def _():
                for part in range(PARTS):
                    second_hop(n, h, part).wait_send()

    for slot in range(2):
        for h in range(2):
            for part in range(PARTS):
                at = pl.ds(part * part_step, part_step)
                ref = o_ref.at[at, pl.ds(slot * tile + h * width, width)]
                recv = y_recv.at[slot, h, part]
                remote(ref, ref, y_send.at[0, 0, 0], recv, mate).wait_recv()


HAND_ON = 4


def hand_on(x_ref, o_ref, held, in_sem, out_sem):
    step = x_ref.shape[0] // HAND_ON

    def copies(n):
        at = pl.ds(n * step, step)
        load = pltpu.make_async_copy(x_ref.at[at], held.at[at], in_sem.at[n])
        return load, pltpu.make_async_copy(held.at[at], o_ref.at[at], out_sem.at[n])

    for n in range(HAND_ON):
        copies(n)[0].start()
    for n in range(HAND_ON):
        copies(n)[0].wait()
        copies(n)[1].start()
    for n in range(HAND_ON):
        copies(n)[1].wait()


def shards(covariance, rotations):
    rows, pair = covariance.shape
    width = rotations.shape[1]
    dma = pltpu.SemaphoreType.DMA
    placed = pl.pallas_call(
        kernel,
        out_shape=jax.ShapeDtypeStruct((rows, pair), BF16),
        in_specs=[pl.BlockSpec(memory_space=pl.ANY)] * 2,
        out_specs=pl.BlockSpec(memory_space=pl.ANY),
        scratch_shapes=[
            pltpu.VMEM((rows, pair), jnp.float32),
            pltpu.VMEM((pair, width), BF16),
            pltpu.VMEM((pair, pair), BF16),
            pltpu.VMEM((pair, pair), BF16),
            pltpu.VMEM((pair, width), BF16),
            pltpu.VMEM((pair, width // 4), BF16),
            pltpu.VMEM((pair, width), BF16),
            pltpu.VMEM((pair, width), BF16),
            pltpu.VMEM((2, 2 * width, width), BF16),
            dma((C_CHUNKS,)),
            dma,
            dma,
            dma((C_CHUNKS,)),
            dma((C_CHUNKS,)),
            dma((C_CHUNKS,)),
            dma((C_CHUNKS,)),
            dma((C_CHUNKS,)),
            dma((C_CHUNKS,)),
            dma,
            dma,
            dma((2,)),
            dma((2,)),
            dma((XS - 1, 2)),
            dma((XS - 1, 2)),
            dma((XS, 2)),
            dma((XS, 2)),
            dma((2, CHUNKS)),
            dma((2, CHUNKS)),
            dma((2, 2, PARTS)),
            dma((2, 2, PARTS)),
            dma((2, 2, PARTS)),
            dma((2, 2, PARTS)),
            dma((2, 2, PARTS)),
        ],
        compiler_params=pltpu.CompilerParams(
            collective_id=0,
            has_side_effects=True,
            vmem_limit_bytes=56 * 1024 * 1024,
        ),
        cost_estimate=pl.CostEstimate(
            flops=4 * rows * pair * pair, bytes_accessed=8 * rows * pair, transcendentals=0
        ),
    )(covariance, rotations)
    return pl.pallas_call(
        hand_on,
        out_shape=jax.ShapeDtypeStruct((rows, pair), BF16),
        in_specs=[pl.BlockSpec(memory_space=pl.ANY)],
        out_specs=pl.BlockSpec(memory_space=pl.ANY),
        scratch_shapes=[
            pltpu.VMEM((rows, pair), BF16),
            dma((HAND_ON,)),
            dma((HAND_ON,)),
        ],
    )(placed)


def solution(mesh):
    placed = (P("row", "col"), P(None, "row"))
    return jax.shard_map(
        shards, mesh=mesh, in_specs=placed, out_specs=P("row", "col"), check_vma=False
    )
```
